32 devices in a mesh: dp: 16 (over z, y, core), mp: 2 (over x).
Axes of the slice: x: 2, y: 2, z: 4, core: 2. Of those that a mesh axis runs over, the one named last changes fastest.
Arguments:
- tokens: bfloat16 [16384, 768], P(('dp', 'mp')), may hold values from -6 to 6
- norm1_gain: bfloat16 [768], replicated, may hold values from 0.25 to 1.75
- qkv_weight: bfloat16 [768, 3, 768], P('dp', None, 'mp'), may hold values from -0.21875 to 0.21875
- attn_out_weight: bfloat16 [768, 768], P('mp', 'dp'), may hold values from -1.75 to 1.75
- bias_table: bfloat16 [32, 12], replicated, may hold values from -4 to 4
- buckets: int32 [2047], replicated, may hold values from 0 to 31
- norm2_gain: bfloat16 [768], replicated, may hold values from 0.25 to 1.75
- router_weight: bfloat16 [768, 16], replicated, may hold values from -0.15917969 to 0.15917969
- routes: int32 [16384, 2], P('dp'), may hold values from 0 to 15, all different within a row; in each aligned block of 1024 rows (0 to 1023, 1024 to 2047, ...) at most 256 rows name the same one
- expert_in_weight: bfloat16 [16, 768, 3072], P('dp', None, 'mp'), may hold values from -0.21875 to 0.21875
- expert_out_weight: bfloat16 [16, 3072, 768], P('dp', 'mp'), may hold values from -0.109375 to 0.109375
- cotangent: bfloat16 [16384, 768], P(('dp', 'mp')), may hold values from -6 to 6
Outputs:
- mixed: bfloat16 [16384, 768], P(('dp', 'mp'))
- grad_tokens: float32 [16384, 768], P(('dp', 'mp'))
- grad_norm1_gain: float32 [768], replicated
- grad_qkv_weight: float32 [768, 3, 768], P('dp', None, 'mp')
- grad_attn_out_weight: float32 [768, 768], P('mp', 'dp')
- grad_bias_table: float32 [32, 12], replicated
- grad_norm2_gain: float32 [768], replicated
- grad_router_weight: float32 [768, 16], replicated
- grad_expert_in_weight: float32 [16, 768, 3072], P('dp', None, 'mp')
- grad_expert_out_weight: float32 [16, 3072, 768], P('dp', 'mp')
The draws below stay inside these ranges and needn't reach their ends.
Inputs may be any that keep to these rules, and one draw needn't show every extreme that they name: `routes`: the two experts of a token differ. In each aligned block of 1024 rows no expert is named by more than 256 rows, and in some blocks one expert is named by exactly 256.
All inputs are finite; a program needn't handle non-finite values.
Results may differ from the reference program's by a relative error of at most 0.015.
Values may be sent and summed in bfloat16 or wider, within the bound.
No kernel may reach another device: no remote copies, remote signals or barrier semaphores. Data moves between devices by JAX's collectives and lax.ppermute only.
A program may use at most 256 MiB of HBM per device.

```python
import math
from functools import partial
import jax
import jax.numpy as jnp
import numpy as np
from jax import lax

MODEL_WIDTH = 768
HEADS = 12
HDIM = 64
EXPERT_HIDDEN = 3072
NBUCKET = 32
BLOCK = 256
LEN = 1024
TOK_DP = 1024
TOKENS = 16384
EXPERTS = 16
CAP = 256
N_DP = 16
N_MP = 2


def set_ends(drawn, own_key, low, largest):
    spot = [jax.random.randint(jax.random.fold_in(own_key, axis), (), 0, length) for axis, length in enumerate(drawn.shape)]
    longest = drawn.shape.index(max(drawn.shape))
    neighbour = spot[:longest] + [(spot[longest] + 1) % drawn.shape[longest]] + spot[longest + 1:]
    return drawn.at[tuple(spot)].set(low).at[tuple(neighbour)].set(largest)


def levels(stream_key, dims, split, least, high):
    factor_of, own = 1.0, jax.random.fold_in(stream_key, 6)
    for position, blocks in split:
        draws = jnp.exp(jax.random.uniform(jax.random.fold_in(own, position), (blocks,), jnp.float32, least / len(split), high / len(split)))
        factor_of = factor_of * jnp.repeat(draws, dims[position] // blocks).reshape([-1 if axis == position else 1 for axis in range(len(dims))])
    return factor_of


def assign_block(own_key, own, number, rows, count, top, reach, slope):
    sequence = jax.random.permutation(own_key, count)
    crowded, ordinary = load_shares(count, rows * top, reach, slope, True), load_shares(count, rows * top, reach, slope, False)
    places = jnp.arange(count)

    def named(lengths, turn):
        used = int((lengths > 0).sum())
        fixed = max(1, used // 4)
        moved = fixed + (places - fixed + turn * (used - fixed)) % max(1, count - fixed)
        return jnp.zeros((count,), jnp.int32).at[sequence[jnp.where(places < fixed, places, moved)]].set(jnp.asarray(lengths, jnp.int32))

    lengths = jnp.where(number % 4 == 0, named(crowded, number // 4), named(ordinary, number - number // 4 - 1))
    mixed = jax.random.permutation(jax.random.fold_in(own, 3), count)
    donor, sink = mixed[0:count // 2 * 2:2], mixed[1:count // 2 * 2:2]
    slack = jnp.minimum(lengths[donor] - 1, reach - lengths[sink]) // 2
    slack = jnp.where((donor == sequence[0]) | (sink == sequence[0]) | (lengths[sink] == 0), 0, jnp.maximum(slack, 0))
    moved = jax.random.randint(jax.random.fold_in(own, 4), (count // 2,), 0, 1 << 20) % (slack + 1)
    lengths = lengths.at[donor].add(-moved).at[sink].add(moved)
    labels = jnp.searchsorted(jnp.cumsum(lengths), jnp.arange(rows * top), side="right").astype(jnp.int32)
    table = labels.reshape(top, rows).T
    table = table[jax.random.permutation(jax.random.fold_in(own, 1), rows)]
    turn = jax.random.randint(jax.random.fold_in(own, 2), (rows, 1), 0, top)
    return jnp.take_along_axis(table, (jnp.arange(top)[None, :] + turn) % top, axis=1)


def load_shares(count, total, reach, lean, full):
    portions = [(1 << 20) // math.isqrt(grade ** lean) + 1 for grade in range(1, count + 1)]
    largest = reach if full else min(reach, max(-(-total // count), total * portions[0] // sum(portions)))
    least = 1 if total - largest >= count - 1 else 0
    given, spare = [largest] + [least] * (count - 1), total - largest - least * (count - 1)
    while spare > 0:
        free = [i for i in range(1, count) if given[i] < largest] or [i for i in range(1, count) if given[i] < reach]
        whole, budget = sum([portions[i] for i in free]), spare
        for i in free:
            addition = min(reach - given[i], max(1, budget * portions[i] // whole), spare)
            given[i] = given[i] + addition
            spare = spare - addition
    return np.array(given)


def gaussian(rng, dims, deviation, reach, split=(), kind=jnp.bfloat16):
    drawn = deviation * jax.random.normal(rng, dims, jnp.float32)
    if split:
        drawn = drawn * levels(rng, dims, split, -0.22, 0.18)
    return jnp.clip(drawn, -reach, reach).astype(kind)


def setup_inputs(seed: int = 0) -> dict:
    key_of = jax.random.split(jax.random.key(seed), 13)
    tokens = gaussian(key_of[0], (TOKENS, MODEL_WIDTH), 1.0, 6.0, ((0, 32),))
    norm1_gain = jnp.clip(1.0 + 0.15 * jax.random.normal(key_of[1], (MODEL_WIDTH,), jnp.float32), 0.25, 1.75).astype(jnp.bfloat16)
    qkv_weight = gaussian(key_of[2], (MODEL_WIDTH, 3, HEADS * HDIM), MODEL_WIDTH ** -0.5, 0.21875, ((0, 16), (2, 2)))
    attn_out_weight = gaussian(key_of[3], (HEADS * HDIM, MODEL_WIDTH), (HEADS * HDIM // 64) ** -0.5, 1.75, ((0, 2), (1, 16)))
    bias_table = gaussian(key_of[4], (NBUCKET, HEADS), 1.0, 4.0)
    buckets = set_ends(jax.random.randint(key_of[5], (2 * LEN - 1,), 0, NBUCKET), jax.random.fold_in(key_of[5], 1), 0, NBUCKET - 1).astype(jnp.int32)
    norm2_gain = jnp.clip(1.0 + 0.15 * jax.random.normal(key_of[6], (MODEL_WIDTH,), jnp.float32), 0.25, 1.75).astype(jnp.bfloat16)
    router_weight = gaussian(key_of[7], (MODEL_WIDTH, EXPERTS), 0.027, 0.15917969)
    routes_keys = jax.random.split(jax.random.fold_in(key_of[8], 1), TOKENS // TOK_DP)
    routes_turns = jax.random.permutation(jax.random.fold_in(key_of[8], 3), TOKENS // TOK_DP)
    routes = jax.vmap(lambda own, number: assign_block(jax.random.fold_in(key_of[8], 2), own, number, TOK_DP, EXPERTS, 2, CAP, 1))(routes_keys, routes_turns).reshape((TOKENS, 2))
    expert_in_weight = gaussian(key_of[9], (EXPERTS, MODEL_WIDTH, EXPERT_HIDDEN), MODEL_WIDTH ** -0.5, 0.21875, ((0, 16), (2, 2)))
    expert_out_weight = gaussian(key_of[10], (EXPERTS, EXPERT_HIDDEN, MODEL_WIDTH), EXPERT_HIDDEN ** -0.5, 0.109375, ((0, 16), (1, 2)))
    cotangent = gaussian(key_of[11], (TOKENS, MODEL_WIDTH), 1.0, 6.0, ((0, 32),))
    return {"tokens": tokens, "norm1_gain": norm1_gain, "qkv_weight": qkv_weight, "attn_out_weight": attn_out_weight, "bias_table": bias_table, "buckets": buckets, "norm2_gain": norm2_gain, "router_weight": router_weight, "routes": routes, "expert_in_weight": expert_in_weight, "expert_out_weight": expert_out_weight, "cotangent": cotangent}


EXACT_PRECISION = lax.Precision.HIGHEST
EPSILON = 1e-06
MASKED = -1e+30

@jax.custom_vjp
def reduced_precision(v):
    return lax.optimization_barrier(v.astype(jnp.bfloat16)).astype(jnp.float32)

@jax.custom_vjp
def reduced_backward(v):
    return v

def low_keep(v):
    return (reduced_precision(v), None)

def low_pass(kept, grad):
    return (grad,)

def back_keep(v):
    return (v, None)

def back_low(kept, grad):
    return (reduced_precision(grad),)
reduced_precision.defvjp(low_keep, low_pass)
reduced_backward.defvjp(back_keep, back_low)

def rms_scale(values):
    return lax.rsqrt(lax.optimization_barrier(jnp.mean(values * values, axis=-1, keepdims=True)) + EPSILON)

def tile_output(queries, first_row, keys_all, values, bias_table, buckets):
    tile_rows = queries.shape[0]
    row_pos = first_row + jnp.arange(tile_rows, dtype=jnp.int32)
    col_pos = jnp.arange(LEN, dtype=jnp.int32)
    bucket_ids = buckets[row_pos[:, None] - col_pos[None, :] + (LEN - 1)]
    rel_bias = jnp.transpose(bias_table[bucket_ids], (2, 0, 1))
    scores = jnp.einsum('qhd,khd->hqk', queries, keys_all, precision=EXACT_PRECISION) * 0.125 + rel_bias
    scores = reduced_backward(scores)
    allowed = col_pos[None, :] // BLOCK <= row_pos[:, None] // BLOCK
    scores = jnp.where(allowed[None], scores, MASKED)
    weights = jax.nn.softmax(scores, axis=-1)
    return jnp.einsum('hqk,khd->qhd', reduced_precision(weights), values, precision=EXACT_PRECISION)

def attend_sequence(queries, keys_all, values, bias_table, buckets):
    tile_rows = min(512, LEN)
    tile_count = LEN // tile_rows
    tiled = queries.reshape(tile_count, tile_rows, queries.shape[1], queries.shape[2])
    starts = jnp.arange(tile_count, dtype=jnp.int32) * tile_rows
    step_fn = jax.checkpoint(lambda packed: tile_output(packed[0], packed[1], keys_all, values, bias_table, buckets))
    return lax.map(step_fn, (tiled, starts)).reshape(LEN, queries.shape[1], queries.shape[2])

def expert_apply(packed):
    rows_in, input_weight, output_weight = packed
    replica_count = reduced_backward(jnp.broadcast_to(rows_in[None], (N_MP,) + rows_in.shape))
    hidden_before_activation = reduced_backward(jnp.einsum('yne,eyz->ynz', replica_count, input_weight.reshape(MODEL_WIDTH, N_MP, EXPERT_HIDDEN // N_MP), precision=EXACT_PRECISION))
    hidden_activation = reduced_precision(jax.nn.gelu(hidden_before_activation))
    partial_output = reduced_backward(reduced_precision(jnp.einsum('kgv,kvj->kgj', hidden_activation, output_weight.reshape(N_MP, EXPERT_HIDDEN // N_MP, MODEL_WIDTH), precision=EXACT_PRECISION)))
    return lax.optimization_barrier(jnp.sum(partial_output, axis=0))

def layer_forward(token_f, norm1_gain, qkv_weight, attn_out_weight, bias_table, norm2_gain, router_weight, expert_in_weight, expert_out_weight, routes, buckets):
    normed = reduced_precision(token_f * rms_scale(token_f) * norm1_gain)
    qkv_vals = reduced_backward(reduced_precision(jnp.einsum('td,dch->tch', normed, qkv_weight, precision=EXACT_PRECISION)))
    seq_total = TOKENS // LEN

    def heads_of(index):
        return qkv_vals[:, index].reshape(seq_total, LEN, HEADS, HDIM)
    attend = jax.checkpoint(lambda packed: attend_sequence(packed[0], packed[1], packed[2], bias_table, buckets))
    attended = lax.map(attend, (heads_of(0), heads_of(1), heads_of(2))).reshape(TOKENS, HEADS * HDIM)
    attended = reduced_backward(reduced_precision(attended))
    mid_stream = token_f + reduced_backward(jnp.dot(attended, attn_out_weight, precision=EXACT_PRECISION))
    moe_in = reduced_precision(mid_stream * rms_scale(mid_stream) * norm2_gain)
    logits = reduced_backward(jnp.dot(moe_in, router_weight, precision=EXACT_PRECISION))
    router_probs = jax.nn.softmax(logits, axis=-1)
    selected = jnp.take_along_axis(router_probs, routes, axis=1)
    gate_vals = selected / lax.optimization_barrier(jnp.sum(selected, axis=1, keepdims=True))
    flat_routes = routes.reshape(-1)
    block_routes = routes.reshape(N_DP, 2 * TOK_DP)
    route_hot = (block_routes[..., None] == jnp.arange(EXPERTS, dtype=jnp.int32)).astype(jnp.int32)
    slot_ranks = lax.optimization_barrier(jnp.sum(jnp.cumsum(route_hot, axis=1) * route_hot, axis=-1)) - 1
    columns = (jnp.arange(N_DP, dtype=jnp.int32)[:, None] * CAP + slot_ranks).reshape(-1).astype(jnp.int32)
    token_ids = jnp.arange(2 * TOKENS, dtype=jnp.int32) // 2
    buffers = jnp.zeros((EXPERTS, N_DP * CAP, MODEL_WIDTH), moe_in.dtype).at[flat_routes, columns].set(moe_in[token_ids])
    expert_out = lax.map(jax.checkpoint(expert_apply), (buffers, expert_in_weight, expert_out_weight))
    picked = expert_out[flat_routes, columns].reshape(TOKENS, 2, MODEL_WIDTH)
    return mid_stream + lax.optimization_barrier(jnp.sum(gate_vals[..., None] * picked, axis=1))

def reference(tokens, norm1_gain, qkv_weight, attn_out_weight, bias_table, buckets, norm2_gain, router_weight, routes, expert_in_weight, expert_out_weight, cotangent):
    floats = tuple((argument.astype(jnp.float32) for argument in (tokens, norm1_gain, qkv_weight, attn_out_weight, bias_table, norm2_gain, router_weight, expert_in_weight, expert_out_weight)))
    forward = partial(layer_forward, routes=routes, buckets=buckets)
    result, backward = jax.vjp(forward, *floats)
    grads = backward(cotangent.astype(jnp.float32))
    return (result.astype(jnp.bfloat16), grads[0], grads[1], grads[2], grads[3], grads[4], grads[5], grads[6], grads[7], grads[8])
```

```python
from functools import partial

import jax
import jax.numpy as jnp
from jax import lax
from jax.experimental import pallas as pl
from jax.experimental.pallas import tpu as pltpu
from jax.sharding import PartitionSpec as P

HDIM = 64
NBUCKET = 32
BLOCK = 256
LANES = 128
EPSILON = 1e-06
MASKED = -1e30
BF = jnp.bfloat16
F32 = jnp.float32
SPAN = 2 * BLOCK


def cost(micros):
    return pl.CostEstimate(flops=int(micros * 1.1e9), bytes_accessed=0, transcendentals=0)


def mm(left, right):
    return jnp.dot(left, right, preferred_element_type=F32)


def mm_t(left, right):
    return lax.dot_general(left, right, (((1,), (1,)), ((), ())), preferred_element_type=F32)


def one_hot(condition):
    return jnp.where(condition, 1.0, 0.0).astype(BF)


def rms_scale(values):
    return lax.rsqrt(jnp.mean(values * values, axis=-1, keepdims=True) + EPSILON)


def flip(values):
    return values.astype(F32).T.astype(BF)


def whole(kernel, outs, scratch, rank, arrays, micros, held=(), limit=56):
    vmem = pl.BlockSpec(memory_space=pltpu.VMEM)
    seen = 1 + len(arrays)

    def body(*refs):
        kernel(*refs[:seen], *refs[seen + len(held) :])

    return pl.pallas_call(
        body,
        out_shape=outs,
        in_specs=[pl.BlockSpec(memory_space=pltpu.SMEM)]
        + [vmem] * len(arrays)
        + [pl.BlockSpec(memory_space=pl.ANY)] * len(held),
        out_specs=[vmem] * len(outs),
        scratch_shapes=scratch,
        compiler_params=pltpu.CompilerParams(vmem_limit_bytes=limit * 1024 * 1024),
        cost_estimate=cost(micros),
    )(rank, *arrays, *held)


def idle_kernel(*refs):
    pass


def after(values, *others):
    anywhere = pl.BlockSpec(memory_space=pl.ANY)
    return pl.pallas_call(
        idle_kernel,
        out_shape=jax.ShapeDtypeStruct(values.shape, values.dtype),
        in_specs=[anywhere] * (1 + len(others)),
        out_specs=anywhere,
        input_output_aliases={0: 0},
    )(values, *others)


def shape(dims, kind):
    return jax.ShapeDtypeStruct(dims, kind)


def first_row(rank, shift, ranks, rows):
    return pl.multiple_of(lax.rem(rank + (shift + ranks), ranks) * rows, rows)


def wanted_slots(rank, slots, group):
    return (lax.broadcasted_iota(jnp.int32, (slots, group), 0) + rank * slots).astype(F32)


def route_kernel(slots, rank_ref, routes_ref, routes_t_ref, by_row_ref, by_col_ref, partner_ref):
    experts, group = by_row_ref.shape
    down = lax.broadcasted_iota(jnp.int32, (group, group), 0)
    across = lax.broadcasted_iota(jnp.int32, (group, group), 1)
    first, second = routes_t_ref[0:1, :], routes_t_ref[1:2, :]
    ids = lax.broadcasted_iota(jnp.int32, (experts, group), 0)
    named = (first == ids) | (second == ids)
    earlier = mm(one_hot(named), one_hot(down < across))
    by_row_ref[...] = jnp.where(named, earlier, -1.0)
    lane = lax.broadcasted_iota(jnp.int32, (group, LANES), 1)
    named_col = (routes_ref[:, 0:1] == lane) | (routes_ref[:, 1:2] == lane)
    earlier_col = mm(one_hot(across < down), one_hot(named_col))
    by_col_ref[...] = jnp.where(named_col, earlier_col, -1.0)
    pair = (first + second).astype(F32)
    wanted = wanted_slots(0, LANES, group) + (rank_ref[0] * slots).astype(F32)

    @pl.loop(0, experts)
    def _(expert):
        pick = one_hot(by_row_ref[pl.ds(expert, 1), :] == wanted)
        partner = jnp.broadcast_to(pair - expert.astype(F32) + 1.0, (16, group)).astype(BF)
        partner_ref[expert] = (mm_t(partner, pick) - 1.0).astype(BF)


def grad_rows_kernel(ranks, rank_ref, by_row_ref, *refs):
    pieces = refs[:ranks]
    rows_ref, grad_all = refs[ranks:]
    rank = rank_ref[0]
    group, own = grad_all.shape[0], pieces[0].shape[0]
    experts, slots, _ = rows_ref.shape
    for shift, piece in enumerate(pieces):
        grad_all[pl.ds(first_row(rank, -shift, ranks, own), own), :] = piece[...]
    wanted = wanted_slots(rank, slots, group)

    @pl.loop(0, experts)
    def _(expert):
        pick = one_hot(by_row_ref[pl.ds(expert, 1), :] == wanted)
        rows_ref[expert] = mm(pick, grad_all[...]).astype(BF)


def bias_tile(offsets, distance, seq_len):
    start = seq_len - BLOCK + BLOCK * distance
    spread = jnp.broadcast_to(offsets[:, start : start + SPAN], (BLOCK, SPAN))
    return pltpu.roll(spread, BLOCK, 1, stride=1, stride_axis=0)[:, :BLOCK]


def spread_heads(pair_t):
    head_row = lax.broadcasted_iota(jnp.int32, pair_t.shape, 0) < HDIM
    zero = jnp.zeros_like(pair_t)
    return jnp.where(head_row, pair_t, zero).astype(BF), jnp.where(head_row, zero, pair_t).astype(BF)


def attend_kernel(ranks, rank_ref, gain_ref, weight_ref, table_ref, buckets_ref, *refs):
    pieces = refs[:ranks]
    qkv_ref, attended_ref, log_ref, offsets_ref, bias = refs[ranks:]
    rank = rank_ref[0]
    own = pieces[0].shape[0]
    seq_len, heads_wide = attended_ref.shape
    tile = min(BLOCK, own)
    gain = gain_ref[...]
    for shift, piece in enumerate(pieces):
        base = first_row(rank, -shift, ranks, own)
        for row in range(0, own, tile):
            token_f = piece[row : row + tile, :].astype(F32)
            normed = (token_f * rms_scale(token_f) * gain).astype(BF)
            qkv_ref[pl.ds(base + row, tile), :] = mm(
                normed, weight_ref[:, : 3 * heads_wide]
            ).astype(BF)
    bucket = lax.broadcasted_iota(jnp.int32, (LANES, 2 * seq_len), 0)
    offsets_ref[...] = mm(table_ref[...], one_hot(bucket == buckets_ref[...]))
    blocks = seq_len // BLOCK

    @pl.loop(0, heads_wide // LANES)
    def _(pair):
        column = pl.multiple_of(pair * LANES, LANES)
        queries = spread_heads(
            (qkv_ref[:, pl.ds(column, LANES)].astype(F32) * 0.125).T
        )
        keys = qkv_ref[:, pl.ds(column + heads_wide, LANES)]
        values_t = flip(qkv_ref[:, pl.ds(column + 2 * heads_wide, LANES)])
        for head in range(2):
            for distance in range(blocks):
                bias[head, distance] = bias_tile(
                    offsets_ref[pl.ds(2 * pair + head, 1), :], distance, seq_len
                )
        for block in range(blocks):
            here = slice(block * BLOCK, (block + 1) * BLOCK)
            both = []
            for head in range(2):
                scores = []
                for other in range(block + 1):
                    there = slice(other * BLOCK, (other + 1) * BLOCK)
                    scores.append(mm(keys[there], queries[head][:, here]) + bias[head, block - other])
                top = jnp.max(scores[0], axis=0, keepdims=True)
                for part in scores[1:]:
                    top = jnp.maximum(top, jnp.max(part, axis=0, keepdims=True))
                total = jnp.zeros((1, BLOCK), F32)
                mixed = jnp.zeros((HDIM, BLOCK), F32)
                for other, part in enumerate(scores):
                    there = slice(other * BLOCK, (other + 1) * BLOCK)
                    exponent = jnp.exp(part - top)
                    total += jnp.sum(exponent, axis=0, keepdims=True)
                    mixed += mm(
                        values_t[head * HDIM : (head + 1) * HDIM, there], exponent.astype(BF)
                    )
                both.append(mixed / total)
                log_ref[pl.ds(2 * pair + head, 1), here] = top + jnp.log(total)
            attended_ref[here, pl.ds(column, LANES)] = jnp.concatenate(both, axis=0).T.astype(BF)


def post_kernel(ranks, chunks, rank_ref, gain_ref, by_row_ref, *refs):
    tokens = refs[:ranks]
    attended = refs[ranks : 2 * ranks]
    weights = refs[2 * ranks : 3 * ranks]
    mid_ref, *rows_refs = refs[3 * ranks : 3 * ranks + 1 + chunks]
    moe_in, turned = refs[3 * ranks + 1 + chunks :]
    rank = rank_ref[0]
    own = tokens[0].shape[0]
    tile = min(BLOCK, own)
    gain = gain_ref[...]
    for index, weight in enumerate(weights):
        turned[index] = flip(weight[...])
    for shift, piece in enumerate(tokens):
        base = first_row(rank, -shift, ranks, own)
        for row in range(0, own, tile):
            mid = piece[row : row + tile, :].astype(F32)
            for index, heads in enumerate(attended):
                mid = mid + mm(heads[pl.ds(base + row, tile), :], turned[index])
            if shift == 0:
                mid_ref[row : row + tile, :] = mid
            moe_in[pl.ds(base + row, tile), :] = (mid * rms_scale(mid) * gain).astype(BF)
    group = moe_in.shape[0]
    experts, slots, _ = rows_refs[0].shape
    wanted = wanted_slots(rank, slots * chunks, group)

    @pl.loop(0, experts)
    def _(expert):
        pick = one_hot(by_row_ref[pl.ds(expert, 1), :] == wanted)
        rows = mm(pick, moe_in[...]).astype(BF)
        for chunk, rows_ref in enumerate(rows_refs):
            rows_ref[expert] = rows[chunk * slots : (chunk + 1) * slots]


def gate_parts(own_id, experts, inputs, router, partner):
    lane = lax.broadcasted_iota(jnp.int32, (inputs.shape[0], LANES), 1)
    logits = jnp.where(lane < experts, mm(inputs, router), MASKED)
    exponent = jnp.exp(logits - jnp.max(logits, axis=-1, keepdims=True))
    probs = exponent / jnp.sum(exponent, axis=-1, keepdims=True)
    is_own, is_partner = lane == own_id, lane == partner
    chosen = jnp.sum(jnp.where(is_own, probs, 0.0), axis=-1, keepdims=True)
    pair = chosen + jnp.sum(jnp.where(is_partner, probs, 0.0), axis=-1, keepdims=True)
    return probs, is_own, is_partner, pair, chosen / pair


def gelu_parts(value):
    square = value * value
    slope = 0.7978845608028654
    curve = 0.7978845608028654 * 0.044715
    tanh = jnp.tanh(value * (slope + curve * square))
    half = 0.5 + 0.5 * tanh
    inner = value * (slope + 3.0 * curve * square)
    return value * half, half + half * (1.0 - tanh) * inner


def expert_kernel(
    steps, experts, first_slot, first, last, carried, ids_ref, rows_ref, grads_ref, partner_ref,
    router_ref, in_ref, in_t_ref, out_ref, out_t_ref, *refs
):
    if first:
        refs = refs[carried:]
        dpart_ref, kept_ref, act_ref, dpre_ref, *refs = refs
    else:
        given_result, given_din, dpart_ref, *refs = refs
        act_ref, dpre_ref, *refs = refs[carried:]
    if last:
        din_ref, route_grad_ref, result_ref, result_acc, din_acc = refs
    else:
        part_result_ref, part_din_ref, result_acc, din_acc = refs
    step = pl.program_id(0)
    own_id = ids_ref[0]
    sources, slots, width = rows_ref.shape
    total = sources * slots
    group = BLOCK // slots

    def group_parts(index):
        some = pl.ds(index * group, group)
        inputs = rows_ref[some].reshape(BLOCK, width)
        grad = grads_ref[some].reshape(BLOCK, width)
        row = lax.broadcasted_iota(jnp.int32, (BLOCK, LANES), 0) % slots + first_slot
        square = row == lax.broadcasted_iota(jnp.int32, (BLOCK, LANES), 1)
        spread = jnp.concatenate(
            [
                jnp.broadcast_to(
                    partner_ref[index * group + i][0:1].astype(F32),
                    (slots, LANES),
                )
                for i in range(group)
            ],
            axis=0,
        )
        partner = jnp.sum(jnp.where(square, spread, 0.0), axis=-1, keepdims=True).astype(jnp.int32)
        return inputs, grad.astype(F32), gate_parts(
            own_id, experts, inputs, router_ref[...], partner
        )

    @pl.when(step == 0)
    def _():
        @pl.loop(0, total // BLOCK)
        def _(index):
            here = pl.ds(pl.multiple_of(index * BLOCK, BLOCK), BLOCK)
            if first:
                inputs, grad, parts = group_parts(index)
                dpart_ref[here, :] = (parts[-1] * grad).astype(BF)
                kept_ref[here, :] = inputs
            result_acc[here, :] = jnp.zeros((BLOCK, width), F32)
            din_acc[here, :] = jnp.zeros((BLOCK, width), F32)

    if not first:
        share = given_result.shape[0]

        @pl.when(step < total // share)
        def _():
            mine = pl.ds(pl.multiple_of(step * share, share), share)
            result_acc[mine, :] += given_result[...].astype(F32)
            din_acc[mine, :] += given_din[...].astype(F32)

    tiles = [slice(row, row + BLOCK) for row in range(0, total, BLOCK)]
    inner = [slice(col, col + BLOCK) for col in range(0, in_ref.shape[2], BLOCK)]
    outer = [slice(col, col + BLOCK) for col in range(0, width, BLOCK)]

    def first_products(t, j):
        some = slice(t.start // slots, t.stop // slots)
        inputs = rows_ref[some].reshape(BLOCK, width)
        return mm(inputs, in_ref[0, :, j]), mm(dpart_ref[t, :], out_t_ref[0, :, j])

    def vector_work(t, j, pre, dact):
        act, slope = gelu_parts(pre)
        act_ref[0, t, j] = act.astype(BF)
        dpre_ref[0, t, j] = (dact * slope).astype(BF)

    def second_products(t, n):
        result_acc[t, n] += mm(act_ref[0, t, :], out_ref[0, :, n])
        din_acc[t, n] += mm(dpre_ref[0, t, :], in_t_ref[0, :, n])

    waiting, ready = None, []
    for t in tiles:
        for j in inner:
            products = first_products(t, j)
            if waiting is not None:
                vector_work(*waiting)
            waiting = (t, j, *products)
            if ready:
                second_products(*ready.pop(0))
        ready += [(t, n) for n in outer]
        while len(ready) > len(outer):
            second_products(*ready.pop(0))
    vector_work(*waiting)
    for item in ready:
        second_products(*item)

    if not last:

        @pl.when(step == steps - 1)
        def _():
            part_result_ref[...] = result_acc[...].astype(BF)
            part_din_ref[...] = din_acc[...].astype(BF)

        return

    @pl.when(step == steps - 1)
    def _():
        route_grad_ref[...] = jnp.zeros_like(route_grad_ref)

        @pl.loop(0, total // BLOCK)
        def _(index):
            here = pl.ds(pl.multiple_of(index * BLOCK, BLOCK), BLOCK)
            some = pl.ds(index * group, group)
            inputs, grad, (probs, is_own, is_partner, pair, gate) = group_parts(index)
            result = result_acc[here, :]
            result_ref[some] = (gate * result).astype(BF).reshape(group, slots, width)
            dgate = jnp.sum(result * grad, axis=-1, keepdims=True)
            shared = dgate * gate
            dprobs = jnp.where(is_own, (dgate - shared) / pair, 0.0) + jnp.where(
                is_partner, -shared / pair, 0.0
            )
            dlogits = probs * (dprobs - jnp.sum(dprobs * probs, axis=-1, keepdims=True))
            high = dlogits.astype(BF)
            din_ref[some] = (
                (din_acc[here, :] + mm_t(high, router_ref[...]))
                .astype(BF)
                .reshape(group, slots, width)
            )
            turned = dlogits.T[: route_grad_ref.shape[0], :]
            high = turned.astype(BF)
            low = (turned - high.astype(F32)).astype(BF)
            route_grad_ref[...] += mm(high, inputs) + mm(low, inputs)


def expert_call(
    ids, rows, grads, partners, router, weights, chunk, chunks, experts, pieces, span, kept, made,
    given, micros,
):
    sources, slots, width = rows.shape
    hidden = weights[0].shape[2]
    all_slots = chunks * slots
    block = min(768, hidden)
    per_piece = hidden // block
    start, stop = span
    first, last = start == 0, stop == pieces
    steps = per_piece * (stop - start)
    total = sources * slots
    route_rows = max(16, experts)

    def still(*dims):
        return pl.BlockSpec(dims, lambda i: (0,) * len(dims), pipeline_mode=pl.Buffered(1))

    def cols(i):
        return start + i // per_piece, 0, i % per_piece

    def lines(i):
        return start + i // per_piece, i % per_piece, 0

    wide = pl.BlockSpec((1, width, block), cols)
    tall = pl.BlockSpec((1, block, width), lines)
    mine = pl.BlockSpec((total, width), lambda i: (chunk, 0), pipeline_mode=pl.Buffered(1))
    columns = pl.BlockSpec((1, total, block), lambda i: (start + i // per_piece, chunk, i % per_piece))
    anywhere = pl.BlockSpec(memory_space=pl.ANY)
    stack = shape((chunks * total, width), BF)
    hidden_stack = shape((pieces, chunks * total, hidden), BF)
    if first:
        carried = [*kept, *made]
        operands = carried
        specs = [anywhere] * len(carried)
        outs, out_specs = [stack, stack, hidden_stack, hidden_stack], [mine, mine, columns, columns]
        aliases = {9 + i: i for i in range(len(carried))}
    else:
        carried = made
        operands = [*given[:2], kept[0], *carried]
        shares = min(steps, 2)
        share = pl.BlockSpec((total // shares, width), lambda i: (jnp.minimum(i, shares - 1), 0))
        specs = [share, share, mine] + [anywhere] * len(carried)
        outs, out_specs = [hidden_stack, hidden_stack], [columns, columns]
        aliases = {12 + i: i for i in range(len(carried))}
    if last:
        results = given[2] if len(given) > 2 else None
        if results is not None:
            carried = [*carried, results]
            operands = [*operands, results]
            specs = [*specs, anywhere]
            aliases[9 + len(operands) - 1] = len(outs) + 2
        outs += [
            shape((sources, slots, width), BF),
            shape((route_rows, width), F32),
            shape((sources, all_slots, width), BF),
        ]
        out_specs += [
            still(sources, slots, width),
            still(route_rows, width),
            pl.BlockSpec(
                (sources, slots, width), lambda i: (0, chunk, 0), pipeline_mode=pl.Buffered(1)
            ),
        ]
    else:
        outs += [shape((total, width), BF)] * 2
        out_specs += [still(total, width)] * 2
    found = pl.pallas_call(
        partial(
            expert_kernel, steps, experts, chunk * slots, first, last, len(carried)
        ),
        grid=(steps,),
        in_specs=[
            pl.BlockSpec(memory_space=pltpu.SMEM),
            still(sources, slots, width),
            pl.BlockSpec(
                (sources, slots, width), lambda i: (0, chunk, 0), pipeline_mode=pl.Buffered(1)
            ),
            still(*partners.shape),
            still(width, LANES),
            wide,
            tall,
            tall,
            wide,
        ]
        + specs,
        out_specs=out_specs,
        out_shape=outs,
        input_output_aliases=aliases,
        scratch_shapes=[pltpu.VMEM((total, width), F32), pltpu.VMEM((total, width), F32)],
        compiler_params=pltpu.CompilerParams(
            dimension_semantics=("arbitrary",), vmem_limit_bytes=60 * 1024 * 1024
        ),
        cost_estimate=cost(micros),
    )(ids, rows, grads, partners, router, *weights, *operands)
    if first:
        return found[:2], found[2:4], found[4:]
    return kept, found[:2], found[2:]


def lay_kernel(columns, parts, carried, *refs):
    plain_ref, turned_ref, *copies = refs[parts + carried :]
    if copies:
        lone_ref, *copies = copies
    start = 0
    for part in refs[:parts]:
        if columns:
            end = start + part.shape[1]
            plain_ref[0, :, start:end] = part[...]
            turned_ref[0, start:end, :] = part[...].T
        else:
            end = start + part.shape[0]
            plain_ref[0, start:end, :] = part[...]
            turned_ref[0, :, start:end] = part[...].T
        start = end
    if copies:
        lone_ref[0] = refs[0][...].T
    start = 0
    for copy in copies:
        if columns:
            copy[...] = refs[0][:, start : start + copy.shape[1]]
            start += copy.shape[1]
        else:
            copy[...] = refs[0][start : start + copy.shape[0], :]
            start += copy.shape[0]


def lay_call(ranks, piece, columns, parts, earlier, micros, lengths=()):
    axis = 1 if columns else 0
    rows, cols = parts[0].shape
    length = sum(part.shape[axis] for part in parts)
    runs = [(rows, run) if columns else (run, cols) for run in lengths]
    rows, cols = (rows, length) if columns else (length, cols)
    vmem = pl.BlockSpec(memory_space=pltpu.VMEM)
    return pl.pallas_call(
        partial(lay_kernel, columns, len(parts), len(earlier)),
        grid=(1,),
        in_specs=[vmem] * len(parts) + [pl.BlockSpec(memory_space=pl.ANY)] * len(earlier),
        out_specs=[
            pl.BlockSpec((1, rows, cols), lambda i: (piece, 0, 0), pipeline_mode=pl.Buffered(1)),
            pl.BlockSpec((1, cols, rows), lambda i: (piece, 0, 0), pipeline_mode=pl.Buffered(1)),
        ]
        + [vmem] * (len(runs) + (1 if runs else 0)),
        out_shape=[shape((ranks, rows, cols), BF), shape((ranks, cols, rows), BF)]
        + ([shape((1, cols, rows), BF)] if runs else [])
        + [shape(run, BF) for run in runs],
        input_output_aliases={len(parts) + i: i for i in range(len(earlier))},
        compiler_params=pltpu.CompilerParams(vmem_limit_bytes=60 * 1024 * 1024),
        cost_estimate=cost(micros),
    )(*parts, *earlier)


def add_kernel(pairs, own_ref, *refs):
    out_ref = refs[-1]
    for index in range(2):

        @pl.when(pl.program_id(0) == index)
        def _():
            total = own_ref[...]
            for pair in range(pairs):
                total = total + refs[2 * pair + index][...].astype(F32)
            out_ref[...] = total


def add_call(own, pairs):
    rows, cols = own.shape
    block = pl.BlockSpec((rows // 2, cols), lambda i: (i, 0))
    half = pl.BlockSpec(
        (rows // 2, cols), lambda i: (0, 0), pipeline_mode=pl.Buffered(1)
    )
    return pl.pallas_call(
        partial(add_kernel, len(pairs)),
        grid=(2,),
        in_specs=[block] + [half] * (2 * len(pairs)),
        out_specs=block,
        out_shape=shape(own.shape, F32),
        compiler_params=pltpu.CompilerParams(
            dimension_semantics=("arbitrary",), vmem_limit_bytes=40 * 1024 * 1024
        ),
        cost_estimate=cost(0),
    )(own, *[part for pair in pairs for part in pair])


def combine_kernel(ranks, chunks, rank_ref, by_col_ref, *refs):
    parts, (own_ref, other_ref, spread) = refs[:chunks], refs[chunks:]
    rank = rank_ref[0]
    own, _ = own_ref.shape
    experts, slots, width = parts[0].shape
    total = experts * slots
    tile = min(BLOCK, own)
    lane = lax.broadcasted_iota(jnp.int32, (LANES, total), 1)
    spread[...] = one_hot(lax.broadcasted_iota(jnp.int32, (LANES, total), 0) == lane // slots)
    slot = lax.broadcasted_iota(jnp.int32, (tile, total), 1) % slots + rank * (chunks * slots)
    wanted = slot.astype(F32)
    for shift in range(ranks):
        base = first_row(rank, shift, ranks, own)

        @pl.loop(0, own // tile)
        def _(index):
            row = pl.multiple_of(index * tile, tile)
            here = by_col_ref[pl.ds(base + row, tile), :].astype(BF)
            found = mm(here, spread[...]) - wanted
            part = jnp.zeros((tile, width), F32)
            for chunk, rows in enumerate(parts):
                pick = one_hot(found == float(chunk * slots))
                part = part + mm(pick, rows[...].reshape(total, width))
            if shift == 0:
                own_ref[pl.ds(row, tile), :] = part
            else:
                other_ref[shift - 1, pl.ds(row, tile), :] = part.astype(BF)


def combine_call(rank, ranks, by_col, parts, own, micros, held=()):
    experts, slots, width = parts[0].shape
    return whole(
        partial(combine_kernel, ranks, len(parts)),
        [shape((own, width), F32), shape((ranks - 1, own, width), BF)],
        [pltpu.VMEM((LANES, experts * slots), BF)],
        rank,
        [by_col, *parts],
        micros,
        held,
    )


def norm_back(values, scale, gain, upstream):
    normed = values * scale
    weighted = upstream * gain
    return scale * (weighted - normed * jnp.mean(weighted * normed, axis=-1, keepdims=True))


def mid_back_kernel(ranks, rank_ref, gain_ref, mid_ref, grad_ref, part_ref, *refs):
    received = refs[: ranks - 1]
    weights = refs[ranks - 1 : 2 * ranks - 1]
    dmid_ref, dbranch_ref, heads_ref, other_heads_ref, gain_grad_ref = refs[2 * ranks - 1 :]
    own = mid_ref.shape[0]
    tile = min(BLOCK, own)
    gain_grad = jnp.zeros(gain_ref.shape, F32)
    for row in range(0, own, tile):
        here = slice(row, row + tile)
        dmoe = part_ref[here, :]
        for piece in received:
            dmoe = dmoe + piece[here, :].astype(F32)
        mid = mid_ref[here, :]
        scale = rms_scale(mid)
        gain_grad += jnp.sum(dmoe * (mid * scale), axis=0, keepdims=True)
        dmid = grad_ref[here, :].astype(F32) + norm_back(mid, scale, gain_ref[...], dmoe)
        dmid_ref[here, :] = dmid
        dbranch = dmid.astype(BF)
        dbranch_ref[here, :] = dbranch
        heads_ref[here, :] = mm(dbranch, weights[0][...]).astype(BF)
        for shift in range(1, ranks):
            other_heads_ref[shift - 1, here, :] = mm(dbranch, weights[ranks - shift][...]).astype(
                BF
            )
    gain_grad_ref[...] = gain_grad


def diagonal_sums(tile):
    padded = jnp.concatenate([tile, jnp.zeros_like(tile)], axis=1)
    half = BLOCK // 2
    while half >= 8:
        padded = padded[:half] + pltpu.roll(padded[half:], SPAN - half, 1)
        half //= 2
    row = lax.broadcasted_iota(jnp.int32, padded.shape, 0)
    for bit in (4, 2, 1):
        padded = jnp.where((row & bit) != 0, pltpu.roll(padded, SPAN - bit, 1), padded)
    return pltpu.roll(jnp.sum(padded, axis=0, keepdims=True), BLOCK, 1)


def attend_back_kernel(
    ranks, head_count, rank_ref, qkv_ref, log_ref, offsets_ref, buckets_ref, *refs
):
    grad_pieces = refs[:ranks]
    dqkv, table_ref, bias, bias_grad, dattended, dkeys, dvalues, offset_grad = refs[ranks:]
    rank = rank_ref[0]
    own, heads_wide = grad_pieces[0].shape
    seq_len = dqkv.shape[0]
    blocks = seq_len // BLOCK
    for shift, piece in enumerate(grad_pieces):
        dattended[pl.ds(first_row(rank, -shift, ranks, own), own), :] = piece[...]
    offset_grad[...] = jnp.zeros_like(offset_grad)
    lane_head = lax.broadcasted_iota(jnp.int32, (1, LANES), 1) < HDIM

    @pl.loop(0, heads_wide // LANES)
    def _(pair):
        column = pl.multiple_of(pair * LANES, LANES)
        queries = (qkv_ref[:, pl.ds(column, LANES)].astype(F32) * 0.125).astype(BF)
        queries_t = spread_heads(queries.astype(F32).T)
        keys = qkv_ref[:, pl.ds(column + heads_wide, LANES)]
        keys_t = flip(keys)
        values = qkv_ref[:, pl.ds(column + 2 * heads_wide, LANES)]
        grads = dattended[:, pl.ds(column, LANES)]
        grads_t = spread_heads(grads.astype(F32).T)
        none = jnp.zeros_like(queries)
        queries_h = (jnp.where(lane_head, queries, none), jnp.where(lane_head, none, queries))
        grads_h = (jnp.where(lane_head, grads, none), jnp.where(lane_head, none, grads))
        for head in range(2):
            for distance in range(blocks):
                bias[head, distance] = bias_tile(
                    offsets_ref[pl.ds(2 * pair + head, 1), :], distance, seq_len
                )
        bias_grad[...] = jnp.zeros_like(bias_grad)
        dkeys[...] = jnp.zeros_like(dkeys)
        dvalues[...] = jnp.zeros_like(dvalues)
        for block in range(blocks):
            here = slice(block * BLOCK, (block + 1) * BLOCK)
            dqueries = []
            for head in range(2):
                log_row = log_ref[pl.ds(2 * pair + head, 1), here]
                weights, dweights = [], []
                overlap = jnp.zeros((1, BLOCK), F32)
                for other in range(block + 1):
                    there = slice(other * BLOCK, (other + 1) * BLOCK)
                    scores = mm(keys[there], queries_t[head][:, here]) + bias[head, block - other]
                    weight = jnp.exp(scores - log_row)
                    dweight = mm(values[there], grads_t[head][:, here])
                    overlap += jnp.sum(weight * dweight, axis=0, keepdims=True)
                    dvalues[there, :] += mm(weight.astype(BF), grads_h[head][here])
                    weights.append(weight)
                    dweights.append(dweight)
                dquery = jnp.zeros((HDIM, BLOCK), F32)
                for other in range(block + 1):
                    there = slice(other * BLOCK, (other + 1) * BLOCK)
                    dscores = weights[other] * (dweights[other] - overlap)
                    bias_grad[head, block - other] += dscores
                    dscores = dscores.astype(BF)
                    dkeys[there, :] += mm(dscores, queries_h[head][here])
                    dquery += mm(keys_t[head * HDIM : (head + 1) * HDIM, there], dscores)
                dqueries.append(dquery)
            dqkv[here, pl.ds(column, LANES)] = (
                jnp.concatenate(dqueries, axis=0).T * 0.125
            ).astype(BF)
        dqkv[:, pl.ds(column + heads_wide, LANES)] = dkeys[...].astype(BF)
        dqkv[:, pl.ds(column + 2 * heads_wide, LANES)] = dvalues[...].astype(BF)
        for head in range(2):
            for distance in range(blocks):
                start = seq_len - BLOCK + BLOCK * distance
                offset_grad[pl.ds(2 * pair + head, 1), start : start + SPAN] += diagonal_sums(
                    bias_grad[head, distance]
                )

    bucket = lax.broadcasted_iota(jnp.int32, (LANES, 2 * seq_len), 0)
    hot = one_hot(bucket == buckets_ref[...])
    high = offset_grad[...].astype(BF)
    rest = offset_grad[...] - high.astype(F32)
    low = rest.astype(BF)
    lowest = (rest - low.astype(F32)).astype(BF)
    table = mm_t(high, hot) + mm_t(low, hot) + mm_t(lowest, hot)
    row = lax.broadcasted_iota(jnp.int32, (16, LANES), 0) - rank * head_count
    placed = jnp.zeros((16, LANES), F32)
    for head in range(head_count):
        placed += jnp.where(row == head, table[head : head + 1, :], 0.0)
    table_ref[...] = placed


def project_grad_kernel(ranks, rank_ref, gain_ref, dqkv, dbranch_ref, *refs):
    tokens, attended_pieces = refs[:ranks], refs[ranks : 2 * ranks]
    grad_ref, normed_t = refs[2 * ranks :]
    rank = rank_ref[0]
    own, width = tokens[0].shape
    heads_wide = attended_pieces[0].shape[1]
    tile = min(BLOCK, own)
    for shift in range(ranks):
        base = first_row(rank, -shift, ranks, own)
        for row in range(0, own, tile):
            token_f = tokens[shift][row : row + tile, :].astype(F32)
            normed = token_f * rms_scale(token_f) * gain_ref[...]
            normed_t[:, pl.ds(base + row, tile)] = normed.T.astype(BF)
    here = pl.ds(first_row(rank, 0, ranks, own), own)
    for row in range(0, width, BLOCK):
        there = slice(row, row + BLOCK)
        grad_ref[there, : 3 * heads_wide] = mm(normed_t[there, :], dqkv[...]).astype(BF)
        dbranch_t = flip(dbranch_ref[:, there])
        for piece, attended in enumerate(attended_pieces):
            first = (3 + piece) * heads_wide
            grad_ref[there, first : first + heads_wide] = mm(dbranch_t, attended[here, :]).astype(BF)


def project_back_kernel(ranks, rank_ref, weight_ref, dqkv, table_ref, *refs):
    tokens = refs[:ranks]
    dnormed_ref, dnormed_other_ref, small_ref, gain_grad, dnormed_all = refs[ranks:]
    rank = rank_ref[0]
    own, width = tokens[0].shape
    columns = dqkv.shape[1]
    tile = min(BLOCK, own)
    gain_grad[...] = jnp.zeros_like(gain_grad)
    for row in range(0, width, BLOCK):
        there = slice(row, row + BLOCK)
        dnormed_all[:, there] = mm_t(dqkv[...], weight_ref[there, :columns])
    for shift in range(ranks):
        base = first_row(rank, -shift, ranks, own)
        for row in range(0, own, tile):
            token_f = tokens[shift][row : row + tile, :].astype(F32)
            plain = token_f * rms_scale(token_f)
            dnormed = dnormed_all[pl.ds(base + row, tile), :]
            gain_grad[...] += jnp.sum(dnormed * plain, axis=0, keepdims=True)
            if shift == 0:
                dnormed_ref[row : row + tile, :] = dnormed
            else:
                dnormed_other_ref[ranks - shift - 1, row : row + tile, :] = dnormed.astype(BF)
    small_ref[...] = jnp.zeros_like(small_ref)
    small_ref[0:1, :] = gain_grad[...]
    small_ref[8:24, 0:LANES] = table_ref[...]


def token_back_kernel(ranks, rank_ref, gain_ref, tokens_ref, dmid_ref, part_ref, *refs):
    received, out_ref = refs[: ranks - 1], refs[ranks - 1]
    own = tokens_ref.shape[0]
    tile = min(BLOCK, own)
    for row in range(0, own, tile):
        here = slice(row, row + tile)
        dnormed = part_ref[here, :]
        for piece in received:
            dnormed = dnormed + piece[here, :].astype(F32)
        token_f = tokens_ref[here, :].astype(F32)
        out_ref[here, :] = dmid_ref[here, :] + norm_back(
            token_f, rms_scale(token_f), gain_ref[...], dnormed
        )


def per_device(
    ranks, tokens, norm1_gain, qkv_weight, attn_out_weight, bias_table, buckets, norm2_gain,
    router_weight, routes, expert_in_weight, expert_out_weight, cotangent,
):
    rank = lax.axis_index("mp").astype(jnp.int32)
    rank_arr = rank.reshape(1)
    own, width = tokens.shape
    group = routes.shape[0]
    experts = router_weight.shape[1]
    slots = 4 * group // experts // ranks
    hidden = expert_in_weight.shape[2]
    heads_true = qkv_weight.shape[2]
    head_count = heads_true // HDIM
    heads_wide = -(-heads_true // LANES) * LANES
    head_rows = 16
    chunks = 2 if slots >= 32 else 1

    def sent(values, shift):
        return lax.ppermute(values, "mp", [(i, (i + shift) % ranks) for i in range(ranks)])

    def pieces(values):
        return [values] + [sent(values, shift) for shift in range(1, ranks)]

    def exchanged(parts):
        return [sent(parts[shift - 1], shift) for shift in range(1, ranks)]

    def to_experts(rows):
        return lax.all_to_all(rows, "dp", split_axis=0, concat_axis=0, tiled=True)

    def everywhere(values, late):
        for axis, size in (("dp", experts), ("mp", ranks)):
            if axis == "mp":
                values = after(values, *late)
            bit = 1
            while bit < size:
                others = range(bit, 4 * bit if 4 * bit <= size else 2 * bit, bit)
                values = values + sum(
                    lax.ppermute(values, axis, [(i, i ^ other) for i in range(size)])
                    for other in others
                )
                bit *= 1 + len(others)
        return values

    pad_heads = heads_wide - heads_true
    gain_one = norm1_gain.astype(F32).reshape(1, width)
    gain_two = norm2_gain.astype(F32).reshape(1, width)
    out_shard = jnp.pad(attn_out_weight.T, ((0, 0), (0, pad_heads)))
    shard = jnp.concatenate(
        [
            jnp.pad(qkv_weight, ((0, 0), (0, 0), (0, pad_heads))).reshape(-1, 3 * heads_wide),
            *pieces(out_shard),
        ],
        axis=1,
    )
    weights = lax.all_gather(shard, "dp", axis=0, tiled=True)
    out_pieces = [
        weights[:, (3 + piece) * heads_wide : (4 + piece) * heads_wide] for piece in range(ranks)
    ]
    grad_pieces = pieces(cotangent)
    token_pieces = pieces(tokens)
    in_own, out_own = expert_in_weight[0], expert_out_weight[0]
    quarter = hidden // 4
    *in_stacks, own_in_t, in_first, in_second, in_third = lay_call(
        ranks, 0, True, [in_own], [], 0, (quarter, 2 * quarter, quarter)
    )
    *out_stacks, own_out_t, out_whole = lay_call(ranks, 0, False, [out_own], [], 0, (hidden,))
    own_stacks = (expert_in_weight, own_in_t, expert_out_weight, own_out_t)
    in_first = pieces(after(in_first, *token_pieces[1:]))
    in_second = pieces(after(in_second, *in_first[1:]))
    table = lax.dynamic_slice_in_dim(bias_table.T, rank * head_count, head_count, 0)
    table = jnp.pad(table, ((0, head_rows - head_count), (0, LANES - NBUCKET)))
    lookup = jnp.concatenate([jnp.full((1,), -1, jnp.int32), buckets]).reshape(1, 2 * group)
    router = jnp.pad(router_weight, ((0, 0), (0, LANES - experts)))

    by_row, by_col, partners = whole(
        partial(route_kernel, slots),
        [shape((experts, group), F32), shape((group, LANES), F32), shape((experts, 16, LANES), BF)],
        [],
        rank_arr,
        [routes, routes.T],
        0,
    )
    partners = to_experts(partners)
    (grad_rows,) = whole(
        partial(grad_rows_kernel, ranks),
        [shape((experts, slots, width), BF)],
        [pltpu.VMEM((group, width), BF)],
        rank_arr,
        [by_row, *grad_pieces],
        9,
        held=[partners, *token_pieces[1:], *in_stacks, *out_stacks],
    )
    grad_rows = to_experts(after(grad_rows, weights, *in_first[1:]))

    qkv, attended, log_sums, offsets = whole(
        partial(attend_kernel, ranks),
        [
            shape((group, 3 * heads_wide), BF),
            shape((group, heads_wide), BF),
            shape((8, group), F32),
            shape((head_rows, 2 * group), F32),
        ],
        [pltpu.VMEM((2, group // BLOCK, BLOCK, BLOCK), F32)],
        rank_arr,
        [gain_one, weights, table, lookup, *token_pieces],
        16,
    )
    attended_pieces = [attended] + pieces(after(attended, *in_second[1:]))[1:]
    in_third = pieces(after(in_third, *attended_pieces[1:]))
    out_whole = pieces(after(out_whole, *in_third[1:]))
    mid, *send_rows = whole(
        partial(post_kernel, ranks, chunks),
        [shape((own, width), F32)] + [shape((experts, slots // chunks, width), BF)] * chunks,
        [pltpu.VMEM((group, width), BF), pltpu.VMEM((ranks, heads_wide, width), BF)],
        rank_arr,
        [gain_two, by_row, *token_pieces, *attended_pieces, *out_pieces],
        12,
    )
    for piece in range(1, ranks):
        in_parts = [in_first[piece], in_second[piece], in_third[piece]]
        in_stacks = lay_call(ranks, piece, True, in_parts, in_stacks, 4)
    expert_rows = [to_experts(after(send_rows[0], grad_rows, *in_third[1:]))]
    for rows in send_rows[1:]:
        expert_rows.append(to_experts(after(rows, *expert_rows, *in_stacks)))
    own_expert = lax.axis_index("dp").astype(jnp.int32).reshape(1)
    kept, made, results, din_rows = [], [], [], []
    route_grad = jnp.zeros((max(16, experts), width), F32)
    for chunk in range(chunks):
        spans = [(0, 1), (1, ranks)] if chunk == 0 and ranks > 1 else [(0, ranks)]
        sums = []
        for span in spans:
            if span[1] == ranks:
                sums = [*(sums or [None, None]), *results]
            if span[0] == 1:
                for piece in range(1, ranks):
                    arrived = after(out_whole[piece], *sums[:2])
                    out_stacks = lay_call(ranks, piece, False, [arrived], out_stacks, 4)
            stacks = own_stacks if span == (0, 1) else (*in_stacks, *out_stacks)
            kept, made, sums = expert_call(
                own_expert, expert_rows[chunk], grad_rows, partners, router, stacks, chunk,
                chunks, experts, ranks, span, kept, made, sums, 4 if len(spans) > 1 else 35,
            )
        din, route_part, *results = sums
        din_rows.append(to_experts(din))
        route_grad = route_grad + route_part
    (dpart, rows_kept), (act, dpre) = kept, made
    (results,) = results

    def rows_dot(left, right):
        return lax.dot_general(left, right, (((0,), (0,)), ((), ())), preferred_element_type=F32)

    upper = [
        rows_dot(rows_kept[:, : width // 2], dpre[j]).astype(BF) for j in range(1, ranks)
    ]
    lower = [
        rows_dot(rows_kept[:, width // 2 :], dpre[j]).astype(BF) for j in range(1, ranks)
    ]
    out_grads = [rows_dot(act[j], dpart).astype(BF) for j in range(1, ranks)]
    firsts = [sent(grad, ranks - 1 - j) for j, grad in enumerate(upper)]
    seconds = [
        sent(after(grad, *firsts), ranks - 1 - j) for j, grad in enumerate(lower)
    ]
    dmoe_own, dmoe_other = combine_call(
        rank_arr, ranks, by_col, din_rows, own, 8, held=[*firsts, *out_grads]
    )
    dmoe_pieces = exchanged(dmoe_other)
    in_own_grad = rows_dot(after(rows_kept, dmoe_own), dpre[0])
    out_own_grad = rows_dot(act[0], after(dpart, dmoe_own))
    dmid, dbranch, dheads, other_dheads, gain_two_grad = whole(
        partial(mid_back_kernel, ranks),
        [
            shape((own, width), F32),
            shape((own, width), BF),
            shape((own, heads_wide), BF),
            shape((ranks - 1, own, heads_wide), BF),
            shape((1, width), F32),
        ],
        [],
        rank_arr,
        [gain_two, mid, cotangent, dmoe_own, *dmoe_pieces, *out_pieces],
        6,
        held=seconds,
    )
    dheads = [dheads, *exchanged(other_dheads)]
    thirds = [
        sent(after(grad[: hidden // 2], *dheads[1:]), ranks - 1 - j)
        for j, grad in enumerate(out_grads)
    ]
    early = jnp.concatenate([jnp.pad(gain_two_grad, ((0, 7), (0, 0))), route_grad], axis=0)
    results = to_experts(after(results, *firsts))

    dqkv, table_grad = whole(
        partial(attend_back_kernel, ranks, head_count),
        [shape((group, 3 * heads_wide), BF), shape((16, LANES), F32)],
        [
            pltpu.VMEM((2, group // BLOCK, BLOCK, BLOCK), F32),
            pltpu.VMEM((2, group // BLOCK, BLOCK, BLOCK), F32),
            pltpu.VMEM((group, heads_wide), BF),
            pltpu.VMEM((group, LANES), F32),
            pltpu.VMEM((group, LANES), F32),
            pltpu.VMEM((head_rows, 2 * group), F32),
        ],
        rank_arr,
        [qkv, log_sums, offsets, lookup, *dheads],
        20,
        held=[in_own_grad, out_own_grad],
    )
    (weight_grad,) = whole(
        partial(project_grad_kernel, ranks),
        [shape((width, (3 + ranks) * heads_wide), BF)],
        [pltpu.VMEM((width, group), BF)],
        rank_arr,
        [gain_one, dqkv, dbranch, *token_pieces, *attended_pieces],
        8,
        held=[results, *thirds],
    )
    core = lax.axis_index("dp") % 2
    shards = weight_grad.reshape(experts // 2, 2, width // experts, -1)
    swapped = lax.ppermute(
        lax.dynamic_index_in_dim(shards, 1 - core, 1, keepdims=False),
        "dp",
        [(i, i ^ 1) for i in range(experts)],
    )
    shards = lax.dynamic_index_in_dim(shards, core, 1, keepdims=False)
    shards = (shards.astype(F32) + swapped.astype(F32)).astype(BF)
    dnormed_own, dnormed_other, small = whole(
        partial(project_back_kernel, ranks),
        [
            shape((own, width), F32),
            shape((ranks - 1, own, width), BF),
            shape((24, width), F32),
        ],
        [pltpu.VMEM((1, width), F32), pltpu.VMEM((group, width), F32)],
        rank_arr,
        [weights, dqkv, table_grad, *token_pieces],
        7,
        held=[weight_grad],
    )
    dnormed_pieces = exchanged(after(dnormed_other, swapped))
    fourths = [
        sent(after(grad[hidden // 2 :], *dnormed_pieces), ranks - 1 - j)
        for j, grad in enumerate(out_grads)
    ]
    shards = lax.all_to_all(
        shards,
        "dp",
        split_axis=0,
        concat_axis=0,
        tiled=True,
        axis_index_groups=[list(range(start, experts, 2)) for start in range(2)],
    )
    (grad_tokens,) = whole(
        partial(token_back_kernel, ranks),
        [shape((own, width), F32)],
        [],
        rank_arr,
        [gain_one, tokens, dmid, dnormed_own, *dnormed_pieces],
        0,
    )

    weight_total = jnp.sum(shards.astype(F32), axis=0)
    qkv_grad = weight_total[:, : 3 * heads_wide].reshape(-1, 3, heads_wide)[:, :, :heads_true]
    out_part = jnp.split(weight_total[:, 3 * heads_wide :], ranks, axis=1)
    attn_out_grad = out_part[0]
    for shift in range(1, ranks):
        attn_out_grad = attn_out_grad + sent(out_part[shift], ranks - shift)
    attn_out_grad = attn_out_grad[:, :heads_true].T

    moe_own, moe_other = combine_call(
        rank_arr, ranks, by_col, [results], own, 0, held=dnormed_pieces
    )
    small = jnp.concatenate([small, early], axis=0)
    moe_pieces = exchanged(moe_other)
    small = everywhere(after(small, moe_own), [*moe_pieces, *fourths])
    mixed = mid + moe_own
    for piece in moe_pieces:
        mixed = mixed + piece.astype(F32)

    in_grad = add_call(in_own_grad, list(zip(firsts, seconds)))
    out_grad = add_call(out_own_grad, list(zip(thirds, fourths)))
    return (
        mixed.astype(BF),
        grad_tokens,
        small[0],
        qkv_grad,
        attn_out_grad,
        small[8 : 8 + bias_table.shape[1], :NBUCKET].T,
        small[24],
        small[32 : 32 + experts].T,
        in_grad[None],
        out_grad[None],
    )


def solution(mesh):
    placed = (
        P(("dp", "mp"), None),
        P(),
        P("dp", None, "mp"),
        P("mp", "dp"),
        P(),
        P(),
        P(),
        P(),
        P("dp", None),
        P("dp", None, "mp"),
        P("dp", "mp", None),
        P(("dp", "mp"), None),
    )
    return jax.shard_map(
        partial(per_device, mesh.shape["mp"]),
        mesh=mesh,
        in_specs=placed,
        out_specs=(
            P(("dp", "mp"), None),
            P(("dp", "mp"), None),
            P(),
            P("dp", None, "mp"),
            P("mp", "dp"),
            P(),
            P(),
            P(),
            P("dp", None, "mp"),
            P("dp", "mp", None),
        ),
        check_vma=False,
    )
```

```python
from functools import partial

import jax
import jax.numpy as jnp
from jax import lax
from jax.experimental import pallas as pl
from jax.experimental.pallas import tpu as pltpu
from jax.sharding import PartitionSpec as P

HDIM = 64
NBUCKET = 32
BLOCK = 256
LANES = 128
EPSILON = 1e-06
MASKED = -1e30
BF = jnp.bfloat16
F32 = jnp.float32
SPAN = 2 * BLOCK


def cost(micros):
    return pl.CostEstimate(flops=int(micros * 1.1e9), bytes_accessed=0, transcendentals=0)


def mm(left, right):
    return jnp.dot(left, right, preferred_element_type=F32)


def mm_t(left, right):
    return lax.dot_general(left, right, (((1,), (1,)), ((), ())), preferred_element_type=F32)


def one_hot(condition):
    return jnp.where(condition, 1.0, 0.0).astype(BF)


def rms_scale(values):
    return lax.rsqrt(jnp.mean(values * values, axis=-1, keepdims=True) + EPSILON)


def flip(values):
    return values.astype(F32).T.astype(BF)


def whole(kernel, outs, scratch, rank, arrays, micros, held=(), limit=56):
    vmem = pl.BlockSpec(memory_space=pltpu.VMEM)
    seen = 1 + len(arrays)

    def body(*refs):
        kernel(*refs[:seen], *refs[seen + len(held) :])

    return pl.pallas_call(
        body,
        out_shape=outs,
        in_specs=[pl.BlockSpec(memory_space=pltpu.SMEM)]
        + [vmem] * len(arrays)
        + [pl.BlockSpec(memory_space=pl.ANY)] * len(held),
        out_specs=[vmem] * len(outs),
        scratch_shapes=scratch,
        compiler_params=pltpu.CompilerParams(vmem_limit_bytes=limit * 1024 * 1024),
        cost_estimate=cost(micros),
    )(rank, *arrays, *held)


def idle_kernel(*refs):
    pass


def after(values, *others):
    anywhere = pl.BlockSpec(memory_space=pl.ANY)
    return pl.pallas_call(
        idle_kernel,
        out_shape=jax.ShapeDtypeStruct(values.shape, values.dtype),
        in_specs=[anywhere] * (1 + len(others)),
        out_specs=anywhere,
        input_output_aliases={0: 0},
    )(values, *others)


def shape(dims, kind):
    return jax.ShapeDtypeStruct(dims, kind)


def first_row(rank, shift, ranks, rows):
    return pl.multiple_of(lax.rem(rank + (shift + ranks), ranks) * rows, rows)


def wanted_slots(rank, slots, group):
    return (lax.broadcasted_iota(jnp.int32, (slots, group), 0) + rank * slots).astype(F32)


def route_kernel(slots, rank_ref, routes_ref, routes_t_ref, by_row_ref, by_col_ref, partner_ref):
    experts, group = by_row_ref.shape
    down = lax.broadcasted_iota(jnp.int32, (group, group), 0)
    across = lax.broadcasted_iota(jnp.int32, (group, group), 1)
    first, second = routes_t_ref[0:1, :], routes_t_ref[1:2, :]
    ids = lax.broadcasted_iota(jnp.int32, (experts, group), 0)
    named = (first == ids) | (second == ids)
    earlier = mm(one_hot(named), one_hot(down < across))
    by_row_ref[...] = jnp.where(named, earlier, -1.0)
    lane = lax.broadcasted_iota(jnp.int32, (group, LANES), 1)
    named_col = (routes_ref[:, 0:1] == lane) | (routes_ref[:, 1:2] == lane)
    earlier_col = mm(one_hot(across < down), one_hot(named_col))
    by_col_ref[...] = jnp.where(named_col, earlier_col, -1.0)
    pair = (first + second).astype(F32)
    wanted = wanted_slots(0, LANES, group) + (rank_ref[0] * slots).astype(F32)

    @pl.loop(0, experts)
    def _(expert):
        pick = one_hot(by_row_ref[pl.ds(expert, 1), :] == wanted)
        partner = jnp.broadcast_to(pair - expert.astype(F32) + 1.0, (16, group)).astype(BF)
        partner_ref[expert] = (mm_t(partner, pick) - 1.0).astype(BF)


def grad_rows_kernel(ranks, rank_ref, by_row_ref, *refs):
    pieces = refs[:ranks]
    rows_ref, grad_all = refs[ranks:]
    rank = rank_ref[0]
    group, own = grad_all.shape[0], pieces[0].shape[0]
    experts, slots, _ = rows_ref.shape
    for shift, piece in enumerate(pieces):
        grad_all[pl.ds(first_row(rank, -shift, ranks, own), own), :] = piece[...]
    wanted = wanted_slots(rank, slots, group)

    @pl.loop(0, experts)
    def _(expert):
        pick = one_hot(by_row_ref[pl.ds(expert, 1), :] == wanted)
        rows_ref[expert] = mm(pick, grad_all[...]).astype(BF)


def bias_tile(offsets, distance, seq_len):
    start = seq_len - BLOCK + BLOCK * distance
    spread = jnp.broadcast_to(offsets[:, start : start + SPAN], (BLOCK, SPAN))
    return pltpu.roll(spread, BLOCK, 1, stride=1, stride_axis=0)[:, :BLOCK]


def spread_heads(pair_t):
    head_row = lax.broadcasted_iota(jnp.int32, pair_t.shape, 0) < HDIM
    zero = jnp.zeros_like(pair_t)
    return jnp.where(head_row, pair_t, zero).astype(BF), jnp.where(head_row, zero, pair_t).astype(BF)


def attend_kernel(ranks, rank_ref, gain_ref, weight_ref, table_ref, buckets_ref, *refs):
    pieces = refs[:ranks]
    qkv_ref, attended_ref, log_ref, offsets_ref, bias = refs[ranks:]
    rank = rank_ref[0]
    own = pieces[0].shape[0]
    seq_len, heads_wide = attended_ref.shape
    tile = min(BLOCK, own)
    gain = gain_ref[...]
    for shift, piece in enumerate(pieces):
        base = first_row(rank, -shift, ranks, own)
        for row in range(0, own, tile):
            token_f = piece[row : row + tile, :].astype(F32)
            normed = (token_f * rms_scale(token_f) * gain).astype(BF)
            qkv_ref[pl.ds(base + row, tile), :] = mm(
                normed, weight_ref[:, : 3 * heads_wide]
            ).astype(BF)
    bucket = lax.broadcasted_iota(jnp.int32, (LANES, 2 * seq_len), 0)
    offsets_ref[...] = mm(table_ref[...], one_hot(bucket == buckets_ref[...]))
    blocks = seq_len // BLOCK

    @pl.loop(0, heads_wide // LANES)
    def _(pair):
        column = pl.multiple_of(pair * LANES, LANES)
        queries = spread_heads(
            (qkv_ref[:, pl.ds(column, LANES)].astype(F32) * 0.125).T
        )
        keys = qkv_ref[:, pl.ds(column + heads_wide, LANES)]
        values_t = flip(qkv_ref[:, pl.ds(column + 2 * heads_wide, LANES)])
        for head in range(2):
            for distance in range(blocks):
                bias[head, distance] = bias_tile(
                    offsets_ref[pl.ds(2 * pair + head, 1), :], distance, seq_len
                )
        for block in range(blocks):
            here = slice(block * BLOCK, (block + 1) * BLOCK)
            both = []
            for head in range(2):
                scores = []
                for other in range(block + 1):
                    there = slice(other * BLOCK, (other + 1) * BLOCK)
                    scores.append(mm(keys[there], queries[head][:, here]) + bias[head, block - other])
                top = jnp.max(scores[0], axis=0, keepdims=True)
                for part in scores[1:]:
                    top = jnp.maximum(top, jnp.max(part, axis=0, keepdims=True))
                total = jnp.zeros((1, BLOCK), F32)
                mixed = jnp.zeros((HDIM, BLOCK), F32)
                for other, part in enumerate(scores):
                    there = slice(other * BLOCK, (other + 1) * BLOCK)
                    exponent = jnp.exp(part - top)
                    total += jnp.sum(exponent, axis=0, keepdims=True)
                    mixed += mm(
                        values_t[head * HDIM : (head + 1) * HDIM, there], exponent.astype(BF)
                    )
                both.append(mixed / total)
                log_ref[pl.ds(2 * pair + head, 1), here] = top + jnp.log(total)
            attended_ref[here, pl.ds(column, LANES)] = jnp.concatenate(both, axis=0).T.astype(BF)


def post_kernel(ranks, chunks, rank_ref, gain_ref, by_row_ref, *refs):
    tokens = refs[:ranks]
    attended = refs[ranks : 2 * ranks]
    weights = refs[2 * ranks : 3 * ranks]
    mid_ref, *rows_refs = refs[3 * ranks : 3 * ranks + 1 + chunks]
    moe_in, turned = refs[3 * ranks + 1 + chunks :]
    rank = rank_ref[0]
    own = tokens[0].shape[0]
    tile = min(BLOCK, own)
    gain = gain_ref[...]
    for index, weight in enumerate(weights):
        turned[index] = flip(weight[...])
    for shift, piece in enumerate(tokens):
        base = first_row(rank, -shift, ranks, own)
        for row in range(0, own, tile):
            mid = piece[row : row + tile, :].astype(F32)
            for index, heads in enumerate(attended):
                mid = mid + mm(heads[pl.ds(base + row, tile), :], turned[index])
            if shift == 0:
                mid_ref[row : row + tile, :] = mid
            moe_in[pl.ds(base + row, tile), :] = (mid * rms_scale(mid) * gain).astype(BF)
    group = moe_in.shape[0]
    experts, slots, _ = rows_refs[0].shape
    wanted = wanted_slots(rank, slots * chunks, group)

    @pl.loop(0, experts)
    def _(expert):
        pick = one_hot(by_row_ref[pl.ds(expert, 1), :] == wanted)
        rows = mm(pick, moe_in[...]).astype(BF)
        for chunk, rows_ref in enumerate(rows_refs):
            rows_ref[expert] = rows[chunk * slots : (chunk + 1) * slots]


def gate_parts(own_id, experts, inputs, router, partner):
    lane = lax.broadcasted_iota(jnp.int32, (inputs.shape[0], LANES), 1)
    logits = jnp.where(lane < experts, mm(inputs, router), MASKED)
    exponent = jnp.exp(logits - jnp.max(logits, axis=-1, keepdims=True))
    probs = exponent / jnp.sum(exponent, axis=-1, keepdims=True)
    is_own, is_partner = lane == own_id, lane == partner
    chosen = jnp.sum(jnp.where(is_own, probs, 0.0), axis=-1, keepdims=True)
    pair = chosen + jnp.sum(jnp.where(is_partner, probs, 0.0), axis=-1, keepdims=True)
    return probs, is_own, is_partner, pair, chosen / pair


def gelu_parts(value):
    square = value * value
    slope = 0.7978845608028654
    curve = 0.7978845608028654 * 0.044715
    tanh = jnp.tanh(value * (slope + curve * square))
    half = 0.5 + 0.5 * tanh
    inner = value * (slope + 3.0 * curve * square)
    return value * half, half + half * (1.0 - tanh) * inner


def expert_kernel(
    steps, experts, first_slot, first, last, carried, ids_ref, rows_ref, grads_ref, partner_ref,
    router_ref, in_ref, in_t_ref, out_ref, out_t_ref, *refs
):
    if first:
        refs = refs[carried:]
        dpart_ref, kept_ref, act_ref, dpre_ref, *refs = refs
    else:
        given_result, given_din, dpart_ref, *refs = refs
        act_ref, dpre_ref, *refs = refs[carried:]
    if last:
        din_ref, route_grad_ref, result_ref, result_acc, din_acc = refs
    else:
        part_result_ref, part_din_ref, result_acc, din_acc = refs
    step = pl.program_id(0)
    own_id = ids_ref[0]
    sources, slots, width = rows_ref.shape
    total = sources * slots
    group = BLOCK // slots

    def group_parts(index):
        some = pl.ds(index * group, group)
        inputs = rows_ref[some].reshape(BLOCK, width)
        grad = grads_ref[some].reshape(BLOCK, width)
        row = lax.broadcasted_iota(jnp.int32, (BLOCK, LANES), 0) % slots + first_slot
        square = row == lax.broadcasted_iota(jnp.int32, (BLOCK, LANES), 1)
        spread = jnp.concatenate(
            [
                jnp.broadcast_to(
                    partner_ref[index * group + i][0:1].astype(F32),
                    (slots, LANES),
                )
                for i in range(group)
            ],
            axis=0,
        )
        partner = jnp.sum(jnp.where(square, spread, 0.0), axis=-1, keepdims=True).astype(jnp.int32)
        return inputs, grad.astype(F32), gate_parts(
            own_id, experts, inputs, router_ref[...], partner
        )

    @pl.when(step == 0)
    def _():
        @pl.loop(0, total // BLOCK)
        def _(index):
            here = pl.ds(pl.multiple_of(index * BLOCK, BLOCK), BLOCK)
            if first:
                inputs, grad, parts = group_parts(index)
                dpart_ref[here, :] = (parts[-1] * grad).astype(BF)
                kept_ref[here, :] = inputs
            result_acc[here, :] = jnp.zeros((BLOCK, width), F32)
            din_acc[here, :] = jnp.zeros((BLOCK, width), F32)

    if not first:
        share = given_result.shape[0]

        @pl.when(step < total // share)
        def _():
            mine = pl.ds(pl.multiple_of(step * share, share), share)
            result_acc[mine, :] += given_result[...].astype(F32)
            din_acc[mine, :] += given_din[...].astype(F32)

    tiles = [slice(row, row + BLOCK) for row in range(0, total, BLOCK)]
    inner = [slice(col, col + BLOCK) for col in range(0, in_ref.shape[2], BLOCK)]
    outer = [slice(col, col + BLOCK) for col in range(0, width, BLOCK)]

    def first_products(t, j):
        some = slice(t.start // slots, t.stop // slots)
        inputs = rows_ref[some].reshape(BLOCK, width)
        return mm(inputs, in_ref[0, :, j]), mm(dpart_ref[t, :], out_t_ref[0, :, j])

    def vector_work(t, j, pre, dact):
        act, slope = gelu_parts(pre)
        act_ref[0, t, j] = act.astype(BF)
        dpre_ref[0, t, j] = (dact * slope).astype(BF)

    def second_products(t, n):
        result_acc[t, n] += mm(act_ref[0, t, :], out_ref[0, :, n])
        din_acc[t, n] += mm(dpre_ref[0, t, :], in_t_ref[0, :, n])

    waiting, ready = None, []
    for t in tiles:
        for j in inner:
            products = first_products(t, j)
            if waiting is not None:
                vector_work(*waiting)
            waiting = (t, j, *products)
            if ready:
                second_products(*ready.pop(0))
        ready += [(t, n) for n in outer]
        while len(ready) > len(outer):
            second_products(*ready.pop(0))
    vector_work(*waiting)
    for item in ready:
        second_products(*item)

    if not last:

        @pl.when(step == steps - 1)
        def _():
            part_result_ref[...] = result_acc[...].astype(BF)
            part_din_ref[...] = din_acc[...].astype(BF)

        return

    @pl.when(step == steps - 1)
    def _():
        route_grad_ref[...] = jnp.zeros_like(route_grad_ref)

        @pl.loop(0, total // BLOCK)
        def _(index):
            here = pl.ds(pl.multiple_of(index * BLOCK, BLOCK), BLOCK)
            some = pl.ds(index * group, group)
            inputs, grad, (probs, is_own, is_partner, pair, gate) = group_parts(index)
            result = result_acc[here, :]
            result_ref[some] = (gate * result).astype(BF).reshape(group, slots, width)
            dgate = jnp.sum(result * grad, axis=-1, keepdims=True)
            shared = dgate * gate
            dprobs = jnp.where(is_own, (dgate - shared) / pair, 0.0) + jnp.where(
                is_partner, -shared / pair, 0.0
            )
            dlogits = probs * (dprobs - jnp.sum(dprobs * probs, axis=-1, keepdims=True))
            high = dlogits.astype(BF)
            din_ref[some] = (
                (din_acc[here, :] + mm_t(high, router_ref[...]))
                .astype(BF)
                .reshape(group, slots, width)
            )
            turned = dlogits.T[: route_grad_ref.shape[0], :]
            high = turned.astype(BF)
            low = (turned - high.astype(F32)).astype(BF)
            route_grad_ref[...] += mm(high, inputs) + mm(low, inputs)


def expert_call(
    ids, rows, grads, partners, router, weights, chunk, chunks, experts, pieces, span, kept, made,
    given, micros,
):
    sources, slots, width = rows.shape
    hidden = weights[0].shape[2]
    all_slots = chunks * slots
    block = min(768, hidden)
    per_piece = hidden // block
    start, stop = span
    first, last = start == 0, stop == pieces
    steps = per_piece * (stop - start)
    total = sources * slots
    route_rows = max(16, experts)

    def still(*dims):
        return pl.BlockSpec(dims, lambda i: (0,) * len(dims), pipeline_mode=pl.Buffered(1))

    def cols(i):
        return start + i // per_piece, 0, i % per_piece

    def lines(i):
        return start + i // per_piece, i % per_piece, 0

    wide = pl.BlockSpec((1, width, block), cols)
    tall = pl.BlockSpec((1, block, width), lines)
    mine = pl.BlockSpec((total, width), lambda i: (chunk, 0), pipeline_mode=pl.Buffered(1))
    columns = pl.BlockSpec((1, total, block), lambda i: (start + i // per_piece, chunk, i % per_piece))
    anywhere = pl.BlockSpec(memory_space=pl.ANY)
    stack = shape((chunks * total, width), BF)
    hidden_stack = shape((pieces, chunks * total, hidden), BF)
    if first:
        carried = [*kept, *made]
        operands = carried
        specs = [anywhere] * len(carried)
        outs, out_specs = [stack, stack, hidden_stack, hidden_stack], [mine, mine, columns, columns]
        aliases = {9 + i: i for i in range(len(carried))}
    else:
        carried = made
        operands = [*given[:2], kept[0], *carried]
        shares = min(steps, 2)
        share = pl.BlockSpec((total // shares, width), lambda i: (jnp.minimum(i, shares - 1), 0))
        specs = [share, share, mine] + [anywhere] * len(carried)
        outs, out_specs = [hidden_stack, hidden_stack], [columns, columns]
        aliases = {12 + i: i for i in range(len(carried))}
    if last:
        results = given[2] if len(given) > 2 else None
        if results is not None:
            carried = [*carried, results]
            operands = [*operands, results]
            specs = [*specs, anywhere]
            aliases[9 + len(operands) - 1] = len(outs) + 2
        outs += [
            shape((sources, slots, width), BF),
            shape((route_rows, width), F32),
            shape((sources, all_slots, width), BF),
        ]
        out_specs += [
            still(sources, slots, width),
            still(route_rows, width),
            pl.BlockSpec(
                (sources, slots, width), lambda i: (0, chunk, 0), pipeline_mode=pl.Buffered(1)
            ),
        ]
    else:
        outs += [shape((total, width), BF)] * 2
        out_specs += [still(total, width)] * 2
    found = pl.pallas_call(
        partial(
            expert_kernel, steps, experts, chunk * slots, first, last, len(carried)
        ),
        grid=(steps,),
        in_specs=[
            pl.BlockSpec(memory_space=pltpu.SMEM),
            still(sources, slots, width),
            pl.BlockSpec(
                (sources, slots, width), lambda i: (0, chunk, 0), pipeline_mode=pl.Buffered(1)
            ),
            still(*partners.shape),
            still(width, LANES),
            wide,
            tall,
            tall,
            wide,
        ]
        + specs,
        out_specs=out_specs,
        out_shape=outs,
        input_output_aliases=aliases,
        scratch_shapes=[pltpu.VMEM((total, width), F32), pltpu.VMEM((total, width), F32)],
        compiler_params=pltpu.CompilerParams(
            dimension_semantics=("arbitrary",), vmem_limit_bytes=60 * 1024 * 1024
        ),
        cost_estimate=cost(micros),
    )(ids, rows, grads, partners, router, *weights, *operands)
    if first:
        return found[:2], found[2:4], found[4:]
    return kept, found[:2], found[2:]


def lay_kernel(columns, parts, carried, *refs):
    plain_ref, turned_ref, *copies = refs[parts + carried :]
    if copies:
        lone_ref, *copies = copies
    start = 0
    for part in refs[:parts]:
        if columns:
            end = start + part.shape[1]
            plain_ref[0, :, start:end] = part[...]
            turned_ref[0, start:end, :] = part[...].T
        else:
            end = start + part.shape[0]
            plain_ref[0, start:end, :] = part[...]
            turned_ref[0, :, start:end] = part[...].T
        start = end
    if copies:
        lone_ref[0] = refs[0][...].T
    start = 0
    for copy in copies:
        if columns:
            copy[...] = refs[0][:, start : start + copy.shape[1]]
            start += copy.shape[1]
        else:
            copy[...] = refs[0][start : start + copy.shape[0], :]
            start += copy.shape[0]


def lay_call(ranks, piece, columns, parts, earlier, micros, lengths=()):
    axis = 1 if columns else 0
    rows, cols = parts[0].shape
    length = sum(part.shape[axis] for part in parts)
    runs = [(rows, run) if columns else (run, cols) for run in lengths]
    rows, cols = (rows, length) if columns else (length, cols)
    vmem = pl.BlockSpec(memory_space=pltpu.VMEM)
    return pl.pallas_call(
        partial(lay_kernel, columns, len(parts), len(earlier)),
        grid=(1,),
        in_specs=[vmem] * len(parts) + [pl.BlockSpec(memory_space=pl.ANY)] * len(earlier),
        out_specs=[
            pl.BlockSpec((1, rows, cols), lambda i: (piece, 0, 0), pipeline_mode=pl.Buffered(1)),
            pl.BlockSpec((1, cols, rows), lambda i: (piece, 0, 0), pipeline_mode=pl.Buffered(1)),
        ]
        + [vmem] * (len(runs) + (1 if runs else 0)),
        out_shape=[shape((ranks, rows, cols), BF), shape((ranks, cols, rows), BF)]
        + ([shape((1, cols, rows), BF)] if runs else [])
        + [shape(run, BF) for run in runs],
        input_output_aliases={len(parts) + i: i for i in range(len(earlier))},
        compiler_params=pltpu.CompilerParams(vmem_limit_bytes=60 * 1024 * 1024),
        cost_estimate=cost(micros),
    )(*parts, *earlier)


def add_kernel(pairs, own_ref, *refs):
    out_ref = refs[-1]
    for index in range(2):

        @pl.when(pl.program_id(0) == index)
        def _():
            total = own_ref[...]
            for pair in range(pairs):
                total = total + refs[2 * pair + index][...].astype(F32)
            out_ref[...] = total


def add_call(own, pairs, held=()):
    rows, cols = own.shape
    block = pl.BlockSpec((rows // 2, cols), lambda i: (i, 0))
    half = pl.BlockSpec(
        (rows // 2, cols), lambda i: (0, 0), pipeline_mode=pl.Buffered(1)
    )
    return pl.pallas_call(
        partial(add_kernel, len(pairs)),
        grid=(2,),
        in_specs=[block]
        + [half] * (2 * len(pairs))
        + [pl.BlockSpec(memory_space=pl.ANY)] * len(held),
        out_specs=block,
        out_shape=shape(own.shape, F32),
        compiler_params=pltpu.CompilerParams(
            dimension_semantics=("arbitrary",), vmem_limit_bytes=40 * 1024 * 1024
        ),
        cost_estimate=cost(0),
    )(own, *[part for pair in pairs for part in pair], *held)


def combine_kernel(ranks, chunks, rank_ref, by_col_ref, *refs):
    parts, (own_ref, other_ref, spread) = refs[:chunks], refs[chunks:]
    rank = rank_ref[0]
    own, _ = own_ref.shape
    experts, slots, width = parts[0].shape
    total = experts * slots
    tile = min(BLOCK, own)
    lane = lax.broadcasted_iota(jnp.int32, (LANES, total), 1)
    spread[...] = one_hot(lax.broadcasted_iota(jnp.int32, (LANES, total), 0) == lane // slots)
    slot = lax.broadcasted_iota(jnp.int32, (tile, total), 1) % slots + rank * (chunks * slots)
    wanted = slot.astype(F32)
    for shift in range(ranks):
        base = first_row(rank, shift, ranks, own)

        @pl.loop(0, own // tile)
        def _(index):
            row = pl.multiple_of(index * tile, tile)
            here = by_col_ref[pl.ds(base + row, tile), :].astype(BF)
            found = mm(here, spread[...]) - wanted
            part = jnp.zeros((tile, width), F32)
            for chunk, rows in enumerate(parts):
                pick = one_hot(found == float(chunk * slots))
                part = part + mm(pick, rows[...].reshape(total, width))
            if shift == 0:
                own_ref[pl.ds(row, tile), :] = part
            else:
                other_ref[shift - 1, pl.ds(row, tile), :] = part.astype(BF)


def combine_call(rank, ranks, by_col, parts, own, micros, held=()):
    experts, slots, width = parts[0].shape
    return whole(
        partial(combine_kernel, ranks, len(parts)),
        [shape((own, width), F32), shape((ranks - 1, own, width), BF)],
        [pltpu.VMEM((LANES, experts * slots), BF)],
        rank,
        [by_col, *parts],
        micros,
        held,
    )


def norm_back(values, scale, gain, upstream):
    normed = values * scale
    weighted = upstream * gain
    return scale * (weighted - normed * jnp.mean(weighted * normed, axis=-1, keepdims=True))


def mid_back_kernel(ranks, rank_ref, gain_ref, mid_ref, grad_ref, part_ref, *refs):
    received = refs[: ranks - 1]
    weights = refs[ranks - 1 : 2 * ranks - 1]
    dmid_ref, dbranch_ref, heads_ref, other_heads_ref, gain_grad_ref = refs[2 * ranks - 1 :]
    own = mid_ref.shape[0]
    tile = min(BLOCK, own)
    gain_grad = jnp.zeros(gain_ref.shape, F32)
    for row in range(0, own, tile):
        here = slice(row, row + tile)
        dmoe = part_ref[here, :]
        for piece in received:
            dmoe = dmoe + piece[here, :].astype(F32)
        mid = mid_ref[here, :]
        scale = rms_scale(mid)
        gain_grad += jnp.sum(dmoe * (mid * scale), axis=0, keepdims=True)
        dmid = grad_ref[here, :].astype(F32) + norm_back(mid, scale, gain_ref[...], dmoe)
        dmid_ref[here, :] = dmid
        dbranch = dmid.astype(BF)
        dbranch_ref[here, :] = dbranch
        heads_ref[here, :] = mm(dbranch, weights[0][...]).astype(BF)
        for shift in range(1, ranks):
            other_heads_ref[shift - 1, here, :] = mm(dbranch, weights[ranks - shift][...]).astype(
                BF
            )
    gain_grad_ref[...] = gain_grad


def diagonal_sums(tile):
    padded = jnp.concatenate([tile, jnp.zeros_like(tile)], axis=1)
    half = BLOCK // 2
    while half >= 8:
        padded = padded[:half] + pltpu.roll(padded[half:], SPAN - half, 1)
        half //= 2
    row = lax.broadcasted_iota(jnp.int32, padded.shape, 0)
    for bit in (4, 2, 1):
        padded = jnp.where((row & bit) != 0, pltpu.roll(padded, SPAN - bit, 1), padded)
    return pltpu.roll(jnp.sum(padded, axis=0, keepdims=True), BLOCK, 1)


def attend_back_kernel(
    ranks, head_count, rank_ref, qkv_ref, log_ref, offsets_ref, buckets_ref, *refs
):
    grad_pieces = refs[:ranks]
    dqkv, table_ref, bias, bias_grad, dattended, dkeys, dvalues, offset_grad = refs[ranks:]
    rank = rank_ref[0]
    own, heads_wide = grad_pieces[0].shape
    seq_len = dqkv.shape[0]
    blocks = seq_len // BLOCK
    for shift, piece in enumerate(grad_pieces):
        dattended[pl.ds(first_row(rank, -shift, ranks, own), own), :] = piece[...]
    offset_grad[...] = jnp.zeros_like(offset_grad)
    lane_head = lax.broadcasted_iota(jnp.int32, (1, LANES), 1) < HDIM

    @pl.loop(0, heads_wide // LANES)
    def _(pair):
        column = pl.multiple_of(pair * LANES, LANES)
        queries = (qkv_ref[:, pl.ds(column, LANES)].astype(F32) * 0.125).astype(BF)
        queries_t = spread_heads(queries.astype(F32).T)
        keys = qkv_ref[:, pl.ds(column + heads_wide, LANES)]
        keys_t = flip(keys)
        values = qkv_ref[:, pl.ds(column + 2 * heads_wide, LANES)]
        grads = dattended[:, pl.ds(column, LANES)]
        grads_t = spread_heads(grads.astype(F32).T)
        none = jnp.zeros_like(queries)
        queries_h = (jnp.where(lane_head, queries, none), jnp.where(lane_head, none, queries))
        grads_h = (jnp.where(lane_head, grads, none), jnp.where(lane_head, none, grads))
        for head in range(2):
            for distance in range(blocks):
                bias[head, distance] = bias_tile(
                    offsets_ref[pl.ds(2 * pair + head, 1), :], distance, seq_len
                )
        bias_grad[...] = jnp.zeros_like(bias_grad)
        dkeys[...] = jnp.zeros_like(dkeys)
        dvalues[...] = jnp.zeros_like(dvalues)
        for block in range(blocks):
            here = slice(block * BLOCK, (block + 1) * BLOCK)
            dqueries = []
            for head in range(2):
                log_row = log_ref[pl.ds(2 * pair + head, 1), here]
                weights, dweights = [], []
                overlap = jnp.zeros((1, BLOCK), F32)
                for other in range(block + 1):
                    there = slice(other * BLOCK, (other + 1) * BLOCK)
                    scores = mm(keys[there], queries_t[head][:, here]) + bias[head, block - other]
                    weight = jnp.exp(scores - log_row)
                    dweight = mm(values[there], grads_t[head][:, here])
                    overlap += jnp.sum(weight * dweight, axis=0, keepdims=True)
                    dvalues[there, :] += mm(weight.astype(BF), grads_h[head][here])
                    weights.append(weight)
                    dweights.append(dweight)
                dquery = jnp.zeros((HDIM, BLOCK), F32)
                for other in range(block + 1):
                    there = slice(other * BLOCK, (other + 1) * BLOCK)
                    dscores = weights[other] * (dweights[other] - overlap)
                    bias_grad[head, block - other] += dscores
                    dscores = dscores.astype(BF)
                    dkeys[there, :] += mm(dscores, queries_h[head][here])
                    dquery += mm(keys_t[head * HDIM : (head + 1) * HDIM, there], dscores)
                dqueries.append(dquery)
            dqkv[here, pl.ds(column, LANES)] = (
                jnp.concatenate(dqueries, axis=0).T * 0.125
            ).astype(BF)
        dqkv[:, pl.ds(column + heads_wide, LANES)] = dkeys[...].astype(BF)
        dqkv[:, pl.ds(column + 2 * heads_wide, LANES)] = dvalues[...].astype(BF)
        for head in range(2):
            for distance in range(blocks):
                start = seq_len - BLOCK + BLOCK * distance
                offset_grad[pl.ds(2 * pair + head, 1), start : start + SPAN] += diagonal_sums(
                    bias_grad[head, distance]
                )

    bucket = lax.broadcasted_iota(jnp.int32, (LANES, 2 * seq_len), 0)
    hot = one_hot(bucket == buckets_ref[...])
    high = offset_grad[...].astype(BF)
    rest = offset_grad[...] - high.astype(F32)
    low = rest.astype(BF)
    lowest = (rest - low.astype(F32)).astype(BF)
    table = mm_t(high, hot) + mm_t(low, hot) + mm_t(lowest, hot)
    row = lax.broadcasted_iota(jnp.int32, (16, LANES), 0) - rank * head_count
    placed = jnp.zeros((16, LANES), F32)
    for head in range(head_count):
        placed += jnp.where(row == head, table[head : head + 1, :], 0.0)
    table_ref[...] = placed


def project_grad_kernel(ranks, rank_ref, gain_ref, dqkv, dbranch_ref, *refs):
    tokens, attended_pieces = refs[:ranks], refs[ranks : 2 * ranks]
    grad_ref, normed_t = refs[2 * ranks :]
    rank = rank_ref[0]
    own, width = tokens[0].shape
    heads_wide = attended_pieces[0].shape[1]
    tile = min(BLOCK, own)
    for shift in range(ranks):
        base = first_row(rank, -shift, ranks, own)
        for row in range(0, own, tile):
            token_f = tokens[shift][row : row + tile, :].astype(F32)
            normed = token_f * rms_scale(token_f) * gain_ref[...]
            normed_t[:, pl.ds(base + row, tile)] = normed.T.astype(BF)
    here = pl.ds(first_row(rank, 0, ranks, own), own)
    for row in range(0, width, BLOCK):
        there = slice(row, row + BLOCK)
        grad_ref[there, : 3 * heads_wide] = mm(normed_t[there, :], dqkv[...]).astype(BF)
        dbranch_t = flip(dbranch_ref[:, there])
        for piece, attended in enumerate(attended_pieces):
            first = (3 + piece) * heads_wide
            grad_ref[there, first : first + heads_wide] = mm(dbranch_t, attended[here, :]).astype(BF)


def project_back_kernel(ranks, rank_ref, weight_ref, dqkv, table_ref, *refs):
    tokens = refs[:ranks]
    dnormed_ref, dnormed_other_ref, small_ref, gain_grad, dnormed_all = refs[ranks:]
    rank = rank_ref[0]
    own, width = tokens[0].shape
    columns = dqkv.shape[1]
    tile = min(BLOCK, own)
    gain_grad[...] = jnp.zeros_like(gain_grad)
    for row in range(0, width, BLOCK):
        there = slice(row, row + BLOCK)
        dnormed_all[:, there] = mm_t(dqkv[...], weight_ref[there, :columns])
    for shift in range(ranks):
        base = first_row(rank, -shift, ranks, own)
        for row in range(0, own, tile):
            token_f = tokens[shift][row : row + tile, :].astype(F32)
            plain = token_f * rms_scale(token_f)
            dnormed = dnormed_all[pl.ds(base + row, tile), :]
            gain_grad[...] += jnp.sum(dnormed * plain, axis=0, keepdims=True)
            if shift == 0:
                dnormed_ref[row : row + tile, :] = dnormed
            else:
                dnormed_other_ref[ranks - shift - 1, row : row + tile, :] = dnormed.astype(BF)
    small_ref[...] = jnp.zeros_like(small_ref)
    small_ref[0:1, :] = gain_grad[...]
    small_ref[8:24, 0:LANES] = table_ref[...]


def token_back_kernel(ranks, rank_ref, gain_ref, tokens_ref, dmid_ref, part_ref, *refs):
    received, out_ref = refs[: ranks - 1], refs[ranks - 1]
    own = tokens_ref.shape[0]
    tile = min(BLOCK, own)
    for row in range(0, own, tile):
        here = slice(row, row + tile)
        dnormed = part_ref[here, :]
        for piece in received:
            dnormed = dnormed + piece[here, :].astype(F32)
        token_f = tokens_ref[here, :].astype(F32)
        out_ref[here, :] = dmid_ref[here, :] + norm_back(
            token_f, rms_scale(token_f), gain_ref[...], dnormed
        )


def per_device(
    ranks, tokens, norm1_gain, qkv_weight, attn_out_weight, bias_table, buckets, norm2_gain,
    router_weight, routes, expert_in_weight, expert_out_weight, cotangent,
):
    rank = lax.axis_index("mp").astype(jnp.int32)
    rank_arr = rank.reshape(1)
    own, width = tokens.shape
    group = routes.shape[0]
    experts = router_weight.shape[1]
    slots = 4 * group // experts // ranks
    hidden = expert_in_weight.shape[2]
    heads_true = qkv_weight.shape[2]
    head_count = heads_true // HDIM
    heads_wide = -(-heads_true // LANES) * LANES
    head_rows = 16
    chunks = 2 if slots >= 32 else 1

    def sent(values, shift):
        return lax.ppermute(values, "mp", [(i, (i + shift) % ranks) for i in range(ranks)])

    def pieces(values):
        return [values] + [sent(values, shift) for shift in range(1, ranks)]

    def exchanged(parts):
        return [sent(parts[shift - 1], shift) for shift in range(1, ranks)]

    def to_experts(rows):
        return lax.all_to_all(rows, "dp", split_axis=0, concat_axis=0, tiled=True)

    def everywhere(values, late):
        for axis, size in (("dp", experts), ("mp", ranks)):
            if axis == "mp":
                values = after(values, *late)
            bit = 1
            while bit < size:
                others = range(bit, 4 * bit if 4 * bit <= size else 2 * bit, bit)
                values = values + sum(
                    lax.ppermute(values, axis, [(i, i ^ other) for i in range(size)])
                    for other in others
                )
                bit *= 1 + len(others)
        return values

    pad_heads = heads_wide - heads_true
    gain_one = norm1_gain.astype(F32).reshape(1, width)
    gain_two = norm2_gain.astype(F32).reshape(1, width)
    out_shard = jnp.pad(attn_out_weight.T, ((0, 0), (0, pad_heads)))
    shard = jnp.concatenate(
        [
            jnp.pad(qkv_weight, ((0, 0), (0, 0), (0, pad_heads))).reshape(-1, 3 * heads_wide),
            *pieces(out_shard),
        ],
        axis=1,
    )
    weights = lax.all_gather(shard, "dp", axis=0, tiled=True)
    out_pieces = [
        weights[:, (3 + piece) * heads_wide : (4 + piece) * heads_wide] for piece in range(ranks)
    ]
    grad_pieces = pieces(cotangent)
    token_pieces = pieces(tokens)
    in_own, out_own = expert_in_weight[0], expert_out_weight[0]
    quarter = hidden // 4
    *in_stacks, own_in_t, in_first, in_second, in_third = lay_call(
        ranks, 0, True, [in_own], [], 0, (quarter, 2 * quarter, quarter)
    )
    *out_stacks, own_out_t, out_whole = lay_call(ranks, 0, False, [out_own], [], 0, (hidden,))
    own_stacks = (expert_in_weight, own_in_t, expert_out_weight, own_out_t)
    in_first = pieces(after(in_first, *token_pieces[1:]))
    in_second = pieces(after(in_second, *in_first[1:]))
    table = lax.dynamic_slice_in_dim(bias_table.T, rank * head_count, head_count, 0)
    table = jnp.pad(table, ((0, head_rows - head_count), (0, LANES - NBUCKET)))
    lookup = jnp.concatenate([jnp.full((1,), -1, jnp.int32), buckets]).reshape(1, 2 * group)
    router = jnp.pad(router_weight, ((0, 0), (0, LANES - experts)))

    by_row, by_col, partners = whole(
        partial(route_kernel, slots),
        [shape((experts, group), F32), shape((group, LANES), F32), shape((experts, 16, LANES), BF)],
        [],
        rank_arr,
        [routes, routes.T],
        0,
    )
    partners = to_experts(partners)
    (grad_rows,) = whole(
        partial(grad_rows_kernel, ranks),
        [shape((experts, slots, width), BF)],
        [pltpu.VMEM((group, width), BF)],
        rank_arr,
        [by_row, *grad_pieces],
        9,
        held=[partners, *token_pieces[1:], *in_stacks, *out_stacks],
    )
    grad_rows = to_experts(after(grad_rows, weights, *in_first[1:]))

    qkv, attended, log_sums, offsets = whole(
        partial(attend_kernel, ranks),
        [
            shape((group, 3 * heads_wide), BF),
            shape((group, heads_wide), BF),
            shape((8, group), F32),
            shape((head_rows, 2 * group), F32),
        ],
        [pltpu.VMEM((2, group // BLOCK, BLOCK, BLOCK), F32)],
        rank_arr,
        [gain_one, weights, table, lookup, *token_pieces],
        16,
    )
    attended_pieces = [attended] + pieces(after(attended, *in_second[1:]))[1:]
    in_third = pieces(after(in_third, *attended_pieces[1:]))
    out_whole = pieces(after(out_whole, *in_third[1:]))
    mid, *send_rows = whole(
        partial(post_kernel, ranks, chunks),
        [shape((own, width), F32)] + [shape((experts, slots // chunks, width), BF)] * chunks,
        [pltpu.VMEM((group, width), BF), pltpu.VMEM((ranks, heads_wide, width), BF)],
        rank_arr,
        [gain_two, by_row, *token_pieces, *attended_pieces, *out_pieces],
        12,
    )
    for piece in range(1, ranks):
        in_parts = [in_first[piece], in_second[piece], in_third[piece]]
        in_stacks = lay_call(ranks, piece, True, in_parts, in_stacks, 4)
    expert_rows = [to_experts(after(send_rows[0], grad_rows, *in_third[1:]))]
    for rows in send_rows[1:]:
        expert_rows.append(to_experts(after(rows, *expert_rows, *in_stacks)))
    own_expert = lax.axis_index("dp").astype(jnp.int32).reshape(1)
    kept, made, results, din_rows = [], [], [], []
    route_grad = jnp.zeros((max(16, experts), width), F32)
    for chunk in range(chunks):
        spans = [(0, 1), (1, ranks)] if chunk == 0 and ranks > 1 else [(0, ranks)]
        sums = []
        for span in spans:
            if span[1] == ranks:
                sums = [*(sums or [None, None]), *results]
            if span[0] == 1:
                for piece in range(1, ranks):
                    arrived = after(out_whole[piece], *sums[:2])
                    out_stacks = lay_call(ranks, piece, False, [arrived], out_stacks, 4)
            stacks = own_stacks if span == (0, 1) else (*in_stacks, *out_stacks)
            kept, made, sums = expert_call(
                own_expert, expert_rows[chunk], grad_rows, partners, router, stacks, chunk,
                chunks, experts, ranks, span, kept, made, sums, 4 if len(spans) > 1 else 35,
            )
        din, route_part, *results = sums
        din_rows.append(to_experts(din))
        route_grad = route_grad + route_part
    (dpart, rows_kept), (act, dpre) = kept, made
    (results,) = results

    def rows_dot(left, right):
        return lax.dot_general(left, right, (((0,), (0,)), ((), ())), preferred_element_type=F32)

    upper = [
        rows_dot(rows_kept[:, : width // 2], dpre[j]).astype(BF) for j in range(1, ranks)
    ]
    lower = [
        rows_dot(rows_kept[:, width // 2 :], dpre[j]).astype(BF) for j in range(1, ranks)
    ]
    out_grads = [rows_dot(act[j], dpart).astype(BF) for j in range(1, ranks)]
    firsts = [sent(grad, ranks - 1 - j) for j, grad in enumerate(upper)]
    seconds = [
        sent(after(grad, *firsts), ranks - 1 - j) for j, grad in enumerate(lower)
    ]
    dmoe_own, dmoe_other = combine_call(
        rank_arr, ranks, by_col, din_rows, own, 8, held=[*firsts, *out_grads]
    )
    dmoe_pieces = exchanged(dmoe_other)
    in_own_grad = rows_dot(after(rows_kept, dmoe_own), dpre[0])
    out_own_grad = rows_dot(act[0], after(dpart, dmoe_own))
    dmid, dbranch, dheads, other_dheads, gain_two_grad = whole(
        partial(mid_back_kernel, ranks),
        [
            shape((own, width), F32),
            shape((own, width), BF),
            shape((own, heads_wide), BF),
            shape((ranks - 1, own, heads_wide), BF),
            shape((1, width), F32),
        ],
        [],
        rank_arr,
        [gain_two, mid, cotangent, dmoe_own, *dmoe_pieces, *out_pieces],
        6,
        held=seconds,
    )
    dheads = [dheads, *exchanged(other_dheads)]
    thirds = [
        sent(after(grad[: hidden // 2], *dheads[1:]), ranks - 1 - j)
        for j, grad in enumerate(out_grads)
    ]
    early = jnp.concatenate([jnp.pad(gain_two_grad, ((0, 7), (0, 0))), route_grad], axis=0)
    results = to_experts(after(results, *firsts))

    dqkv, table_grad = whole(
        partial(attend_back_kernel, ranks, head_count),
        [shape((group, 3 * heads_wide), BF), shape((16, LANES), F32)],
        [
            pltpu.VMEM((2, group // BLOCK, BLOCK, BLOCK), F32),
            pltpu.VMEM((2, group // BLOCK, BLOCK, BLOCK), F32),
            pltpu.VMEM((group, heads_wide), BF),
            pltpu.VMEM((group, LANES), F32),
            pltpu.VMEM((group, LANES), F32),
            pltpu.VMEM((head_rows, 2 * group), F32),
        ],
        rank_arr,
        [qkv, log_sums, offsets, lookup, *dheads],
        20,
        held=[in_own_grad, out_own_grad],
    )
    (weight_grad,) = whole(
        partial(project_grad_kernel, ranks),
        [shape((width, (3 + ranks) * heads_wide), BF)],
        [pltpu.VMEM((width, group), BF)],
        rank_arr,
        [gain_one, dqkv, dbranch, *token_pieces, *attended_pieces],
        8,
        held=[results, *thirds],
    )
    core = lax.axis_index("dp") % 2
    shards = weight_grad.reshape(experts // 2, 2, width // experts, -1)
    swapped = lax.ppermute(
        lax.dynamic_index_in_dim(shards, 1 - core, 1, keepdims=False),
        "dp",
        [(i, i ^ 1) for i in range(experts)],
    )
    shards = lax.dynamic_index_in_dim(shards, core, 1, keepdims=False)
    shards = (shards.astype(F32) + swapped.astype(F32)).astype(BF)
    dnormed_own, dnormed_other, small = whole(
        partial(project_back_kernel, ranks),
        [
            shape((own, width), F32),
            shape((ranks - 1, own, width), BF),
            shape((24, width), F32),
        ],
        [pltpu.VMEM((1, width), F32), pltpu.VMEM((group, width), F32)],
        rank_arr,
        [weights, dqkv, table_grad, *token_pieces],
        7,
        held=[weight_grad],
    )
    dnormed_pieces = exchanged(after(dnormed_other, swapped))
    fourths = [
        sent(after(grad[hidden // 2 :], *dnormed_pieces), ranks - 1 - j)
        for j, grad in enumerate(out_grads)
    ]
    shards = lax.all_to_all(
        shards,
        "dp",
        split_axis=0,
        concat_axis=0,
        tiled=True,
        axis_index_groups=[list(range(start, experts, 2)) for start in range(2)],
    )
    (grad_tokens,) = whole(
        partial(token_back_kernel, ranks),
        [shape((own, width), F32)],
        [],
        rank_arr,
        [gain_one, tokens, dmid, dnormed_own, *dnormed_pieces],
        0,
    )

    weight_total = jnp.sum(shards.astype(F32), axis=0)
    qkv_grad = weight_total[:, : 3 * heads_wide].reshape(-1, 3, heads_wide)[:, :, :heads_true]
    out_part = jnp.split(weight_total[:, 3 * heads_wide :], ranks, axis=1)
    out_part = out_part[:1] + [
        sent(out_part[shift], ranks - shift) for shift in range(1, ranks)
    ]
    attn_out_grad = sum(out_part)[:, :heads_true].T

    moe_own, moe_other = combine_call(
        rank_arr, ranks, by_col, [results], own, 0, held=dnormed_pieces
    )
    small = jnp.concatenate([small, early], axis=0)
    moe_pieces = exchanged(moe_other)
    small = everywhere(after(small, moe_own), [*moe_pieces, *fourths])
    mixed = mid + moe_own
    for piece in moe_pieces:
        mixed = mixed + piece.astype(F32)

    in_grad = add_call(in_own_grad, list(zip(firsts, seconds)))
    out_grad = add_call(out_own_grad, list(zip(thirds, fourths)), out_part[1:])
    return (
        mixed.astype(BF),
        grad_tokens,
        small[0],
        qkv_grad,
        attn_out_grad,
        small[8 : 8 + bias_table.shape[1], :NBUCKET].T,
        small[24],
        small[32 : 32 + experts].T,
        in_grad[None],
        out_grad[None],
    )


def solution(mesh):
    placed = (
        P(("dp", "mp"), None),
        P(),
        P("dp", None, "mp"),
        P("mp", "dp"),
        P(),
        P(),
        P(),
        P(),
        P("dp", None),
        P("dp", None, "mp"),
        P("dp", "mp", None),
        P(("dp", "mp"), None),
    )
    return jax.shard_map(
        partial(per_device, mesh.shape["mp"]),
        mesh=mesh,
        in_specs=placed,
        out_specs=(
            P(("dp", "mp"), None),
            P(("dp", "mp"), None),
            P(),
            P("dp", None, "mp"),
            P("mp", "dp"),
            P(),
            P(),
            P(),
            P("dp", None, "mp"),
            P("dp", "mp", None),
        ),
        check_vma=False,
    )
```

```python
from functools import partial

import jax
import jax.numpy as jnp
from jax import lax
from jax.experimental import pallas as pl
from jax.experimental.pallas import tpu as pltpu
from jax.sharding import PartitionSpec as P

HDIM = 64
NBUCKET = 32
BLOCK = 256
LANES = 128
EPSILON = 1e-06
MASKED = -1e30
BF = jnp.bfloat16
F32 = jnp.float32
SPAN = 2 * BLOCK


def cost(micros):
    return pl.CostEstimate(flops=int(micros * 1.1e9), bytes_accessed=0, transcendentals=0)


def mm(left, right):
    return jnp.dot(left, right, preferred_element_type=F32)


def mm_t(left, right):
    return lax.dot_general(left, right, (((1,), (1,)), ((), ())), preferred_element_type=F32)


def one_hot(condition):
    return jnp.where(condition, 1.0, 0.0).astype(BF)


def rms_scale(values):
    return lax.rsqrt(jnp.mean(values * values, axis=-1, keepdims=True) + EPSILON)


def flip(values):
    return values.astype(F32).T.astype(BF)


def whole(kernel, outs, scratch, rank, arrays, micros, held=(), limit=56):
    vmem = pl.BlockSpec(memory_space=pltpu.VMEM)
    seen = 1 + len(arrays)

    def body(*refs):
        kernel(*refs[:seen], *refs[seen + len(held) :])

    return pl.pallas_call(
        body,
        out_shape=outs,
        in_specs=[pl.BlockSpec(memory_space=pltpu.SMEM)]
        + [vmem] * len(arrays)
        + [pl.BlockSpec(memory_space=pl.ANY)] * len(held),
        out_specs=[vmem] * len(outs),
        scratch_shapes=scratch,
        compiler_params=pltpu.CompilerParams(vmem_limit_bytes=limit * 1024 * 1024),
        cost_estimate=cost(micros),
    )(rank, *arrays, *held)


def idle_kernel(*refs):
    pass


def after(values, *others):
    anywhere = pl.BlockSpec(memory_space=pl.ANY)
    return pl.pallas_call(
        idle_kernel,
        out_shape=jax.ShapeDtypeStruct(values.shape, values.dtype),
        in_specs=[anywhere] * (1 + len(others)),
        out_specs=anywhere,
        input_output_aliases={0: 0},
    )(values, *others)


def shape(dims, kind):
    return jax.ShapeDtypeStruct(dims, kind)


def first_row(rank, shift, ranks, rows):
    return pl.multiple_of(lax.rem(rank + (shift + ranks), ranks) * rows, rows)


def wanted_slots(rank, slots, group):
    return (lax.broadcasted_iota(jnp.int32, (slots, group), 0) + rank * slots).astype(F32)


def route_kernel(slots, rank_ref, routes_ref, routes_t_ref, by_row_ref, by_col_ref, partner_ref):
    experts, group = by_row_ref.shape
    down = lax.broadcasted_iota(jnp.int32, (group, group), 0)
    across = lax.broadcasted_iota(jnp.int32, (group, group), 1)
    first, second = routes_t_ref[0:1, :], routes_t_ref[1:2, :]
    ids = lax.broadcasted_iota(jnp.int32, (experts, group), 0)
    named = (first == ids) | (second == ids)
    earlier = mm(one_hot(named), one_hot(down < across))
    by_row_ref[...] = jnp.where(named, earlier, -1.0)
    lane = lax.broadcasted_iota(jnp.int32, (group, LANES), 1)
    named_col = (routes_ref[:, 0:1] == lane) | (routes_ref[:, 1:2] == lane)
    earlier_col = mm(one_hot(across < down), one_hot(named_col))
    by_col_ref[...] = jnp.where(named_col, earlier_col, -1.0)
    pair = (first + second).astype(F32)
    wanted = wanted_slots(0, LANES, group) + (rank_ref[0] * slots).astype(F32)

    @pl.loop(0, experts)
    def _(expert):
        pick = one_hot(by_row_ref[pl.ds(expert, 1), :] == wanted)
        partner = jnp.broadcast_to(pair - expert.astype(F32) + 1.0, (16, group)).astype(BF)
        partner_ref[expert] = (mm_t(partner, pick) - 1.0).astype(BF)


def grad_rows_kernel(ranks, rank_ref, by_row_ref, *refs):
    pieces = refs[:ranks]
    rows_ref, grad_all = refs[ranks:]
    rank = rank_ref[0]
    group, own = grad_all.shape[0], pieces[0].shape[0]
    experts, slots, _ = rows_ref.shape
    for shift, piece in enumerate(pieces):
        grad_all[pl.ds(first_row(rank, -shift, ranks, own), own), :] = piece[...]
    wanted = wanted_slots(rank, slots, group)

    @pl.loop(0, experts)
    def _(expert):
        pick = one_hot(by_row_ref[pl.ds(expert, 1), :] == wanted)
        rows_ref[expert] = mm(pick, grad_all[...]).astype(BF)


def bias_tile(offsets, distance, seq_len):
    start = seq_len - BLOCK + BLOCK * distance
    spread = jnp.broadcast_to(offsets[:, start : start + SPAN], (BLOCK, SPAN))
    return pltpu.roll(spread, BLOCK, 1, stride=1, stride_axis=0)[:, :BLOCK]


def spread_heads(pair_t):
    head_row = lax.broadcasted_iota(jnp.int32, pair_t.shape, 0) < HDIM
    zero = jnp.zeros_like(pair_t)
    return jnp.where(head_row, pair_t, zero).astype(BF), jnp.where(head_row, zero, pair_t).astype(BF)


def attend_kernel(ranks, rank_ref, gain_ref, weight_ref, table_ref, buckets_ref, *refs):
    pieces = refs[:ranks]
    qkv_ref, attended_ref, log_ref, offsets_ref, bias = refs[ranks:]
    rank = rank_ref[0]
    own = pieces[0].shape[0]
    seq_len, heads_wide = attended_ref.shape
    tile = min(BLOCK, own)
    gain = gain_ref[...]
    for shift, piece in enumerate(pieces):
        base = first_row(rank, -shift, ranks, own)
        for row in range(0, own, tile):
            token_f = piece[row : row + tile, :].astype(F32)
            normed = (token_f * rms_scale(token_f) * gain).astype(BF)
            qkv_ref[pl.ds(base + row, tile), :] = mm(
                normed, weight_ref[:, : 3 * heads_wide]
            ).astype(BF)
    bucket = lax.broadcasted_iota(jnp.int32, (LANES, 2 * seq_len), 0)
    offsets_ref[...] = mm(table_ref[...], one_hot(bucket == buckets_ref[...]))
    blocks = seq_len // BLOCK

    @pl.loop(0, heads_wide // LANES)
    def _(pair):
        column = pl.multiple_of(pair * LANES, LANES)
        queries = spread_heads(
            (qkv_ref[:, pl.ds(column, LANES)].astype(F32) * 0.125).T
        )
        keys = qkv_ref[:, pl.ds(column + heads_wide, LANES)]
        values_t = flip(qkv_ref[:, pl.ds(column + 2 * heads_wide, LANES)])
        for head in range(2):
            for distance in range(blocks):
                bias[head, distance] = bias_tile(
                    offsets_ref[pl.ds(2 * pair + head, 1), :], distance, seq_len
                )
        for block in range(blocks):
            here = slice(block * BLOCK, (block + 1) * BLOCK)
            both = []
            for head in range(2):
                scores = []
                for other in range(block + 1):
                    there = slice(other * BLOCK, (other + 1) * BLOCK)
                    scores.append(mm(keys[there], queries[head][:, here]) + bias[head, block - other])
                top = jnp.max(scores[0], axis=0, keepdims=True)
                for part in scores[1:]:
                    top = jnp.maximum(top, jnp.max(part, axis=0, keepdims=True))
                total = jnp.zeros((1, BLOCK), F32)
                mixed = jnp.zeros((HDIM, BLOCK), F32)
                for other, part in enumerate(scores):
                    there = slice(other * BLOCK, (other + 1) * BLOCK)
                    exponent = jnp.exp(part - top)
                    total += jnp.sum(exponent, axis=0, keepdims=True)
                    mixed += mm(
                        values_t[head * HDIM : (head + 1) * HDIM, there], exponent.astype(BF)
                    )
                both.append(mixed / total)
                log_ref[pl.ds(2 * pair + head, 1), here] = top + jnp.log(total)
            attended_ref[here, pl.ds(column, LANES)] = jnp.concatenate(both, axis=0).T.astype(BF)


def post_kernel(ranks, chunks, rank_ref, gain_ref, by_row_ref, *refs):
    tokens = refs[:ranks]
    attended = refs[ranks : 2 * ranks]
    weights = refs[2 * ranks : 3 * ranks]
    mid_ref, *rows_refs = refs[3 * ranks : 3 * ranks + 1 + chunks]
    moe_in, turned = refs[3 * ranks + 1 + chunks :]
    rank = rank_ref[0]
    own = tokens[0].shape[0]
    tile = min(BLOCK, own)
    gain = gain_ref[...]
    for index, weight in enumerate(weights):
        turned[index] = flip(weight[...])
    for shift, piece in enumerate(tokens):
        base = first_row(rank, -shift, ranks, own)
        for row in range(0, own, tile):
            mid = piece[row : row + tile, :].astype(F32)
            for index, heads in enumerate(attended):
                mid = mid + mm(heads[pl.ds(base + row, tile), :], turned[index])
            if shift == 0:
                mid_ref[row : row + tile, :] = mid
            moe_in[pl.ds(base + row, tile), :] = (mid * rms_scale(mid) * gain).astype(BF)
    group = moe_in.shape[0]
    experts, slots, _ = rows_refs[0].shape
    wanted = wanted_slots(rank, slots * chunks, group)

    @pl.loop(0, experts)
    def _(expert):
        pick = one_hot(by_row_ref[pl.ds(expert, 1), :] == wanted)
        rows = mm(pick, moe_in[...]).astype(BF)
        for chunk, rows_ref in enumerate(rows_refs):
            rows_ref[expert] = rows[chunk * slots : (chunk + 1) * slots]


def gate_parts(own_id, experts, inputs, router, partner):
    lane = lax.broadcasted_iota(jnp.int32, (inputs.shape[0], LANES), 1)
    logits = jnp.where(lane < experts, mm(inputs, router), MASKED)
    exponent = jnp.exp(logits - jnp.max(logits, axis=-1, keepdims=True))
    probs = exponent / jnp.sum(exponent, axis=-1, keepdims=True)
    is_own, is_partner = lane == own_id, lane == partner
    chosen = jnp.sum(jnp.where(is_own, probs, 0.0), axis=-1, keepdims=True)
    pair = chosen + jnp.sum(jnp.where(is_partner, probs, 0.0), axis=-1, keepdims=True)
    return probs, is_own, is_partner, pair, chosen / pair


def gelu_parts(value):
    square = value * value
    slope = 0.7978845608028654
    curve = 0.7978845608028654 * 0.044715
    tanh = jnp.tanh(value * (slope + curve * square))
    half = 0.5 + 0.5 * tanh
    inner = value * (slope + 3.0 * curve * square)
    return value * half, half + half * (1.0 - tanh) * inner


def expert_kernel(
    steps, experts, first_slot, first, last, carried, ids_ref, rows_ref, grads_ref, partner_ref,
    router_ref, in_ref, in_t_ref, out_ref, out_t_ref, *refs
):
    if first:
        refs = refs[carried:]
        dpart_ref, kept_ref, act_ref, dpre_ref, *refs = refs
    else:
        given_result, given_din, dpart_ref, *refs = refs
        act_ref, dpre_ref, *refs = refs[carried:]
    if last:
        din_ref, route_grad_ref, result_ref, result_acc, din_acc = refs
    else:
        part_result_ref, part_din_ref, result_acc, din_acc = refs
    step = pl.program_id(0)
    own_id = ids_ref[0]
    sources, slots, width = rows_ref.shape
    total = sources * slots
    group = BLOCK // slots

    def group_parts(index):
        some = pl.ds(index * group, group)
        inputs = rows_ref[some].reshape(BLOCK, width)
        grad = grads_ref[some].reshape(BLOCK, width)
        row = lax.broadcasted_iota(jnp.int32, (BLOCK, LANES), 0) % slots + first_slot
        square = row == lax.broadcasted_iota(jnp.int32, (BLOCK, LANES), 1)
        spread = jnp.concatenate(
            [
                jnp.broadcast_to(
                    partner_ref[index * group + i][0:1].astype(F32),
                    (slots, LANES),
                )
                for i in range(group)
            ],
            axis=0,
        )
        partner = jnp.sum(jnp.where(square, spread, 0.0), axis=-1, keepdims=True).astype(jnp.int32)
        return inputs, grad.astype(F32), gate_parts(
            own_id, experts, inputs, router_ref[...], partner
        )

    @pl.when(step == 0)
    def _():
        @pl.loop(0, total // BLOCK)
        def _(index):
            here = pl.ds(pl.multiple_of(index * BLOCK, BLOCK), BLOCK)
            if first:
                inputs, grad, parts = group_parts(index)
                dpart_ref[here, :] = (parts[-1] * grad).astype(BF)
                kept_ref[here, :] = inputs
            result_acc[here, :] = jnp.zeros((BLOCK, width), F32)
            din_acc[here, :] = jnp.zeros((BLOCK, width), F32)

    if not first:
        share = given_result.shape[0]

        @pl.when(step < total // share)
        def _():
            mine = pl.ds(pl.multiple_of(step * share, share), share)
            result_acc[mine, :] += given_result[...].astype(F32)
            din_acc[mine, :] += given_din[...].astype(F32)

    tiles = [slice(row, row + BLOCK) for row in range(0, total, BLOCK)]
    inner = [slice(col, col + BLOCK) for col in range(0, in_ref.shape[2], BLOCK)]
    outer = [slice(col, col + BLOCK) for col in range(0, width, BLOCK)]

    def first_products(t, j):
        some = slice(t.start // slots, t.stop // slots)
        inputs = rows_ref[some].reshape(BLOCK, width)
        return mm(inputs, in_ref[0, :, j]), mm(dpart_ref[t, :], out_t_ref[0, :, j])

    def vector_work(t, j, pre, dact):
        act, slope = gelu_parts(pre)
        act_ref[0, t, j] = act.astype(BF)
        dpre_ref[0, t, j] = (dact * slope).astype(BF)

    def second_products(t, n):
        result_acc[t, n] += mm(act_ref[0, t, :], out_ref[0, :, n])
        din_acc[t, n] += mm(dpre_ref[0, t, :], in_t_ref[0, :, n])

    waiting, ready = None, []
    for t in tiles:
        for j in inner:
            products = first_products(t, j)
            if waiting is not None:
                vector_work(*waiting)
            waiting = (t, j, *products)
            if ready:
                second_products(*ready.pop(0))
        ready += [(t, n) for n in outer]
        while len(ready) > len(outer):
            second_products(*ready.pop(0))
    vector_work(*waiting)
    for item in ready:
        second_products(*item)

    if not last:

        @pl.when(step == steps - 1)
        def _():
            part_result_ref[...] = result_acc[...].astype(BF)
            part_din_ref[...] = din_acc[...].astype(BF)

        return

    @pl.when(step == steps - 1)
    def _():
        route_grad_ref[...] = jnp.zeros_like(route_grad_ref)

        @pl.loop(0, total // BLOCK)
        def _(index):
            here = pl.ds(pl.multiple_of(index * BLOCK, BLOCK), BLOCK)
            some = pl.ds(index * group, group)
            inputs, grad, (probs, is_own, is_partner, pair, gate) = group_parts(index)
            result = result_acc[here, :]
            result_ref[some] = (gate * result).astype(BF).reshape(group, slots, width)
            dgate = jnp.sum(result * grad, axis=-1, keepdims=True)
            shared = dgate * gate
            dprobs = jnp.where(is_own, (dgate - shared) / pair, 0.0) + jnp.where(
                is_partner, -shared / pair, 0.0
            )
            dlogits = probs * (dprobs - jnp.sum(dprobs * probs, axis=-1, keepdims=True))
            high = dlogits.astype(BF)
            din_ref[some] = (
                (din_acc[here, :] + mm_t(high, router_ref[...]))
                .astype(BF)
                .reshape(group, slots, width)
            )
            turned = dlogits.T[: route_grad_ref.shape[0], :]
            high = turned.astype(BF)
            low = (turned - high.astype(F32)).astype(BF)
            route_grad_ref[...] += mm(high, inputs) + mm(low, inputs)


def expert_call(
    ids, rows, grads, partners, router, weights, chunk, chunks, experts, pieces, span, kept, made,
    given, micros,
):
    sources, slots, width = rows.shape
    hidden = weights[0].shape[2]
    all_slots = chunks * slots
    block = min(768, hidden)
    per_piece = hidden // block
    start, stop = span
    first, last = start == 0, stop == pieces
    steps = per_piece * (stop - start)
    total = sources * slots
    route_rows = max(16, experts)

    def still(*dims):
        return pl.BlockSpec(dims, lambda i: (0,) * len(dims), pipeline_mode=pl.Buffered(1))

    def cols(i):
        return start + i // per_piece, 0, i % per_piece

    def lines(i):
        return start + i // per_piece, i % per_piece, 0

    wide = pl.BlockSpec((1, width, block), cols)
    tall = pl.BlockSpec((1, block, width), lines)
    mine = pl.BlockSpec((total, width), lambda i: (chunk, 0), pipeline_mode=pl.Buffered(1))
    columns = pl.BlockSpec((1, total, block), lambda i: (start + i // per_piece, chunk, i % per_piece))
    anywhere = pl.BlockSpec(memory_space=pl.ANY)
    stack = shape((chunks * total, width), BF)
    hidden_stack = shape((pieces, chunks * total, hidden), BF)
    if first:
        carried = [*kept, *made]
        operands = carried
        specs = [anywhere] * len(carried)
        outs, out_specs = [stack, stack, hidden_stack, hidden_stack], [mine, mine, columns, columns]
        aliases = {9 + i: i for i in range(len(carried))}
    else:
        carried = made
        operands = [*given[:2], kept[0], *carried]
        shares = min(steps, 2)
        share = pl.BlockSpec((total // shares, width), lambda i: (jnp.minimum(i, shares - 1), 0))
        specs = [share, share, mine] + [anywhere] * len(carried)
        outs, out_specs = [hidden_stack, hidden_stack], [columns, columns]
        aliases = {12 + i: i for i in range(len(carried))}
    if last:
        results = given[2] if len(given) > 2 else None
        if results is not None:
            carried = [*carried, results]
            operands = [*operands, results]
            specs = [*specs, anywhere]
            aliases[9 + len(operands) - 1] = len(outs) + 2
        outs += [
            shape((sources, slots, width), BF),
            shape((route_rows, width), F32),
            shape((sources, all_slots, width), BF),
        ]
        out_specs += [
            still(sources, slots, width),
            still(route_rows, width),
            pl.BlockSpec(
                (sources, slots, width), lambda i: (0, chunk, 0), pipeline_mode=pl.Buffered(1)
            ),
        ]
    else:
        outs += [shape((total, width), BF)] * 2
        out_specs += [still(total, width)] * 2
    found = pl.pallas_call(
        partial(
            expert_kernel, steps, experts, chunk * slots, first, last, len(carried)
        ),
        grid=(steps,),
        in_specs=[
            pl.BlockSpec(memory_space=pltpu.SMEM),
            still(sources, slots, width),
            pl.BlockSpec(
                (sources, slots, width), lambda i: (0, chunk, 0), pipeline_mode=pl.Buffered(1)
            ),
            still(*partners.shape),
            still(width, LANES),
            wide,
            tall,
            tall,
            wide,
        ]
        + specs,
        out_specs=out_specs,
        out_shape=outs,
        input_output_aliases=aliases,
        scratch_shapes=[pltpu.VMEM((total, width), F32), pltpu.VMEM((total, width), F32)],
        compiler_params=pltpu.CompilerParams(
            dimension_semantics=("arbitrary",), vmem_limit_bytes=60 * 1024 * 1024
        ),
        cost_estimate=cost(micros),
    )(ids, rows, grads, partners, router, *weights, *operands)
    if first:
        return found[:2], found[2:4], found[4:]
    return kept, found[:2], found[2:]


def lay_kernel(columns, parts, carried, *refs):
    plain_ref, turned_ref, *copies = refs[parts + carried :]
    if copies:
        lone_ref, *copies = copies
    start = 0
    for part in refs[:parts]:
        if columns:
            end = start + part.shape[1]
            plain_ref[0, :, start:end] = part[...]
            turned_ref[0, start:end, :] = part[...].T
        else:
            end = start + part.shape[0]
            plain_ref[0, start:end, :] = part[...]
            turned_ref[0, :, start:end] = part[...].T
        start = end
    if copies:
        lone_ref[0] = refs[0][...].T
    start = 0
    for copy in copies:
        if columns:
            copy[...] = refs[0][:, start : start + copy.shape[1]]
            start += copy.shape[1]
        else:
            copy[...] = refs[0][start : start + copy.shape[0], :]
            start += copy.shape[0]


def lay_call(ranks, piece, columns, parts, earlier, micros, lengths=()):
    axis = 1 if columns else 0
    rows, cols = parts[0].shape
    length = sum(part.shape[axis] for part in parts)
    runs = [(rows, run) if columns else (run, cols) for run in lengths]
    rows, cols = (rows, length) if columns else (length, cols)
    vmem = pl.BlockSpec(memory_space=pltpu.VMEM)
    return pl.pallas_call(
        partial(lay_kernel, columns, len(parts), len(earlier)),
        grid=(1,),
        in_specs=[vmem] * len(parts) + [pl.BlockSpec(memory_space=pl.ANY)] * len(earlier),
        out_specs=[
            pl.BlockSpec((1, rows, cols), lambda i: (piece, 0, 0), pipeline_mode=pl.Buffered(1)),
            pl.BlockSpec((1, cols, rows), lambda i: (piece, 0, 0), pipeline_mode=pl.Buffered(1)),
        ]
        + [vmem] * (len(runs) + (1 if runs else 0)),
        out_shape=[shape((ranks, rows, cols), BF), shape((ranks, cols, rows), BF)]
        + ([shape((1, cols, rows), BF)] if runs else [])
        + [shape(run, BF) for run in runs],
        input_output_aliases={len(parts) + i: i for i in range(len(earlier))},
        compiler_params=pltpu.CompilerParams(vmem_limit_bytes=60 * 1024 * 1024),
        cost_estimate=cost(micros),
    )(*parts, *earlier)


def add_kernel(places, own_ref, *refs):
    out_ref = refs[-1]
    half = own_ref.shape[0]
    for index in range(2):

        @pl.when(pl.program_id(0) == index)
        def _():
            out_ref[...] = own_ref[...]
            for (first, last), ref in zip(places, refs):
                start, stop = max(first, index * half), min(last, (index + 1) * half)
                if start < stop:
                    out_ref[start - index * half : stop - index * half, :] += ref[
                        start - first : stop - first, :
                    ].astype(F32)


def add_call(own, groups):
    rows, cols = own.shape
    half = rows // 2
    places, parts = [], []
    for group in groups:
        start = 0
        for part in group:
            places.append((start, start + part.shape[0]))
            parts.append(part)
            start += part.shape[0]
    block = pl.BlockSpec((half, cols), lambda i: (i, 0))
    return pl.pallas_call(
        partial(add_kernel, places),
        grid=(2,),
        in_specs=[block]
        + [
            pl.BlockSpec(part.shape, lambda i: (0, 0), pipeline_mode=pl.Buffered(1))
            for part in parts
        ],
        out_specs=block,
        out_shape=shape(own.shape, F32),
        compiler_params=pltpu.CompilerParams(
            dimension_semantics=("arbitrary",), vmem_limit_bytes=40 * 1024 * 1024
        ),
        cost_estimate=cost(0),
    )(own, *parts)


def combine_kernel(ranks, chunks, rank_ref, by_col_ref, *refs):
    parts, (own_ref, other_ref, spread) = refs[:chunks], refs[chunks:]
    rank = rank_ref[0]
    own, _ = own_ref.shape
    experts, slots, width = parts[0].shape
    total = experts * slots
    tile = min(BLOCK, own)
    lane = lax.broadcasted_iota(jnp.int32, (LANES, total), 1)
    spread[...] = one_hot(lax.broadcasted_iota(jnp.int32, (LANES, total), 0) == lane // slots)
    slot = lax.broadcasted_iota(jnp.int32, (tile, total), 1) % slots + rank * (chunks * slots)
    wanted = slot.astype(F32)
    for shift in range(ranks):
        base = first_row(rank, shift, ranks, own)

        @pl.loop(0, own // tile)
        def _(index):
            row = pl.multiple_of(index * tile, tile)
            here = by_col_ref[pl.ds(base + row, tile), :].astype(BF)
            found = mm(here, spread[...]) - wanted
            part = jnp.zeros((tile, width), F32)
            for chunk, rows in enumerate(parts):
                pick = one_hot(found == float(chunk * slots))
                part = part + mm(pick, rows[...].reshape(total, width))
            if shift == 0:
                own_ref[pl.ds(row, tile), :] = part
            else:
                other_ref[shift - 1, pl.ds(row, tile), :] = part.astype(BF)


def combine_call(rank, ranks, by_col, parts, own, micros, held=()):
    experts, slots, width = parts[0].shape
    return whole(
        partial(combine_kernel, ranks, len(parts)),
        [shape((own, width), F32), shape((ranks - 1, own, width), BF)],
        [pltpu.VMEM((LANES, experts * slots), BF)],
        rank,
        [by_col, *parts],
        micros,
        held,
    )


def norm_back(values, scale, gain, upstream):
    normed = values * scale
    weighted = upstream * gain
    return scale * (weighted - normed * jnp.mean(weighted * normed, axis=-1, keepdims=True))


def mid_back_kernel(ranks, rank_ref, gain_ref, mid_ref, grad_ref, part_ref, *refs):
    received = refs[: ranks - 1]
    weights = refs[ranks - 1 : 2 * ranks - 1]
    dmid_ref, dbranch_ref, heads_ref, other_heads_ref, gain_grad_ref = refs[2 * ranks - 1 :]
    own = mid_ref.shape[0]
    tile = min(BLOCK, own)
    gain_grad = jnp.zeros(gain_ref.shape, F32)
    for row in range(0, own, tile):
        here = slice(row, row + tile)
        dmoe = part_ref[here, :]
        for piece in received:
            dmoe = dmoe + piece[here, :].astype(F32)
        mid = mid_ref[here, :]
        scale = rms_scale(mid)
        gain_grad += jnp.sum(dmoe * (mid * scale), axis=0, keepdims=True)
        dmid = grad_ref[here, :].astype(F32) + norm_back(mid, scale, gain_ref[...], dmoe)
        dmid_ref[here, :] = dmid
        dbranch = dmid.astype(BF)
        dbranch_ref[here, :] = dbranch
        heads_ref[here, :] = mm(dbranch, weights[0][...]).astype(BF)
        for shift in range(1, ranks):
            other_heads_ref[shift - 1, here, :] = mm(dbranch, weights[ranks - shift][...]).astype(
                BF
            )
    gain_grad_ref[...] = gain_grad


def diagonal_sums(tile):
    padded = jnp.concatenate([tile, jnp.zeros_like(tile)], axis=1)
    half = BLOCK // 2
    while half >= 8:
        padded = padded[:half] + pltpu.roll(padded[half:], SPAN - half, 1)
        half //= 2
    row = lax.broadcasted_iota(jnp.int32, padded.shape, 0)
    for bit in (4, 2, 1):
        padded = jnp.where((row & bit) != 0, pltpu.roll(padded, SPAN - bit, 1), padded)
    return pltpu.roll(jnp.sum(padded, axis=0, keepdims=True), BLOCK, 1)


def attend_back_kernel(
    ranks, head_count, rank_ref, qkv_ref, log_ref, offsets_ref, buckets_ref, *refs
):
    grad_pieces = refs[:ranks]
    dqkv, table_ref, bias, bias_grad, dattended, dkeys, dvalues, offset_grad = refs[ranks:]
    rank = rank_ref[0]
    own, heads_wide = grad_pieces[0].shape
    seq_len = dqkv.shape[0]
    blocks = seq_len // BLOCK
    for shift, piece in enumerate(grad_pieces):
        dattended[pl.ds(first_row(rank, -shift, ranks, own), own), :] = piece[...]
    offset_grad[...] = jnp.zeros_like(offset_grad)
    lane_head = lax.broadcasted_iota(jnp.int32, (1, LANES), 1) < HDIM

    @pl.loop(0, heads_wide // LANES)
    def _(pair):
        column = pl.multiple_of(pair * LANES, LANES)
        queries = (qkv_ref[:, pl.ds(column, LANES)].astype(F32) * 0.125).astype(BF)
        queries_t = spread_heads(queries.astype(F32).T)
        keys = qkv_ref[:, pl.ds(column + heads_wide, LANES)]
        keys_t = flip(keys)
        values = qkv_ref[:, pl.ds(column + 2 * heads_wide, LANES)]
        grads = dattended[:, pl.ds(column, LANES)]
        grads_t = spread_heads(grads.astype(F32).T)
        none = jnp.zeros_like(queries)
        queries_h = (jnp.where(lane_head, queries, none), jnp.where(lane_head, none, queries))
        grads_h = (jnp.where(lane_head, grads, none), jnp.where(lane_head, none, grads))
        for head in range(2):
            for distance in range(blocks):
                bias[head, distance] = bias_tile(
                    offsets_ref[pl.ds(2 * pair + head, 1), :], distance, seq_len
                )
        bias_grad[...] = jnp.zeros_like(bias_grad)
        dkeys[...] = jnp.zeros_like(dkeys)
        dvalues[...] = jnp.zeros_like(dvalues)
        for block in range(blocks):
            here = slice(block * BLOCK, (block + 1) * BLOCK)
            dqueries = []
            for head in range(2):
                log_row = log_ref[pl.ds(2 * pair + head, 1), here]
                weights, dweights = [], []
                overlap = jnp.zeros((1, BLOCK), F32)
                for other in range(block + 1):
                    there = slice(other * BLOCK, (other + 1) * BLOCK)
                    scores = mm(keys[there], queries_t[head][:, here]) + bias[head, block - other]
                    weight = jnp.exp(scores - log_row)
                    dweight = mm(values[there], grads_t[head][:, here])
                    overlap += jnp.sum(weight * dweight, axis=0, keepdims=True)
                    dvalues[there, :] += mm(weight.astype(BF), grads_h[head][here])
                    weights.append(weight)
                    dweights.append(dweight)
                dquery = jnp.zeros((HDIM, BLOCK), F32)
                for other in range(block + 1):
                    there = slice(other * BLOCK, (other + 1) * BLOCK)
                    dscores = weights[other] * (dweights[other] - overlap)
                    bias_grad[head, block - other] += dscores
                    dscores = dscores.astype(BF)
                    dkeys[there, :] += mm(dscores, queries_h[head][here])
                    dquery += mm(keys_t[head * HDIM : (head + 1) * HDIM, there], dscores)
                dqueries.append(dquery)
            dqkv[here, pl.ds(column, LANES)] = (
                jnp.concatenate(dqueries, axis=0).T * 0.125
            ).astype(BF)
        dqkv[:, pl.ds(column + heads_wide, LANES)] = dkeys[...].astype(BF)
        dqkv[:, pl.ds(column + 2 * heads_wide, LANES)] = dvalues[...].astype(BF)
        for head in range(2):
            for distance in range(blocks):
                start = seq_len - BLOCK + BLOCK * distance
                offset_grad[pl.ds(2 * pair + head, 1), start : start + SPAN] += diagonal_sums(
                    bias_grad[head, distance]
                )

    bucket = lax.broadcasted_iota(jnp.int32, (LANES, 2 * seq_len), 0)
    hot = one_hot(bucket == buckets_ref[...])
    high = offset_grad[...].astype(BF)
    rest = offset_grad[...] - high.astype(F32)
    low = rest.astype(BF)
    lowest = (rest - low.astype(F32)).astype(BF)
    table = mm_t(high, hot) + mm_t(low, hot) + mm_t(lowest, hot)
    row = lax.broadcasted_iota(jnp.int32, (16, LANES), 0) - rank * head_count
    placed = jnp.zeros((16, LANES), F32)
    for head in range(head_count):
        placed += jnp.where(row == head, table[head : head + 1, :], 0.0)
    table_ref[...] = placed


def project_grad_kernel(ranks, rank_ref, gain_ref, dqkv, dbranch_ref, *refs):
    tokens, attended_pieces = refs[:ranks], refs[ranks : 2 * ranks]
    grad_ref, normed_t = refs[2 * ranks :]
    rank = rank_ref[0]
    own, width = tokens[0].shape
    heads_wide = attended_pieces[0].shape[1]
    tile = min(BLOCK, own)
    for shift in range(ranks):
        base = first_row(rank, -shift, ranks, own)
        for row in range(0, own, tile):
            token_f = tokens[shift][row : row + tile, :].astype(F32)
            normed = token_f * rms_scale(token_f) * gain_ref[...]
            normed_t[:, pl.ds(base + row, tile)] = normed.T.astype(BF)
    here = pl.ds(first_row(rank, 0, ranks, own), own)
    for row in range(0, width, BLOCK):
        there = slice(row, row + BLOCK)
        grad_ref[there, : 3 * heads_wide] = mm(normed_t[there, :], dqkv[...]).astype(BF)
        dbranch_t = flip(dbranch_ref[:, there])
        for piece, attended in enumerate(attended_pieces):
            first = (3 + piece) * heads_wide
            grad_ref[there, first : first + heads_wide] = mm(dbranch_t, attended[here, :]).astype(BF)


def project_back_kernel(ranks, rank_ref, weight_ref, dqkv, table_ref, *refs):
    tokens = refs[:ranks]
    dnormed_ref, dnormed_other_ref, small_ref, gain_grad, dnormed_all = refs[ranks:]
    rank = rank_ref[0]
    own, width = tokens[0].shape
    columns = dqkv.shape[1]
    tile = min(BLOCK, own)
    gain_grad[...] = jnp.zeros_like(gain_grad)
    for row in range(0, width, BLOCK):
        there = slice(row, row + BLOCK)
        dnormed_all[:, there] = mm_t(dqkv[...], weight_ref[there, :columns])
    for shift in range(ranks):
        base = first_row(rank, -shift, ranks, own)
        for row in range(0, own, tile):
            token_f = tokens[shift][row : row + tile, :].astype(F32)
            plain = token_f * rms_scale(token_f)
            dnormed = dnormed_all[pl.ds(base + row, tile), :]
            gain_grad[...] += jnp.sum(dnormed * plain, axis=0, keepdims=True)
            if shift == 0:
                dnormed_ref[row : row + tile, :] = dnormed
            else:
                dnormed_other_ref[ranks - shift - 1, row : row + tile, :] = dnormed.astype(BF)
    small_ref[...] = jnp.zeros_like(small_ref)
    small_ref[0:1, :] = gain_grad[...]
    small_ref[8:24, 0:LANES] = table_ref[...]


def back_and_grad_kernel(ranks, head_count, rank_ref, qkv_ref, log_ref, offsets_ref, *refs):
    buckets_ref, heads, refs = refs[0], refs[1 : 1 + ranks], refs[1 + ranks :]
    gain_ref, dbranch_ref, pieces, refs = refs[0], refs[1], refs[2 : 2 + 2 * ranks], refs[2 + 2 * ranks :]
    dqkv, table_ref, grad_ref, *scratch, normed_t = refs
    attend_back_kernel(
        ranks, head_count, rank_ref, qkv_ref, log_ref, offsets_ref, buckets_ref, *heads, dqkv,
        table_ref, *scratch,
    )
    project_grad_kernel(ranks, rank_ref, gain_ref, dqkv, dbranch_ref, *pieces, grad_ref, normed_t)


def token_back_kernel(ranks, rank_ref, gain_ref, tokens_ref, dmid_ref, part_ref, *refs):
    received, out_ref = refs[: ranks - 1], refs[ranks - 1]
    own = tokens_ref.shape[0]
    tile = min(BLOCK, own)
    for row in range(0, own, tile):
        here = slice(row, row + tile)
        dnormed = part_ref[here, :]
        for piece in received:
            dnormed = dnormed + piece[here, :].astype(F32)
        token_f = tokens_ref[here, :].astype(F32)
        out_ref[here, :] = dmid_ref[here, :] + norm_back(
            token_f, rms_scale(token_f), gain_ref[...], dnormed
        )


def per_device(
    ranks, tokens, norm1_gain, qkv_weight, attn_out_weight, bias_table, buckets, norm2_gain,
    router_weight, routes, expert_in_weight, expert_out_weight, cotangent,
):
    rank = lax.axis_index("mp").astype(jnp.int32)
    rank_arr = rank.reshape(1)
    own, width = tokens.shape
    group = routes.shape[0]
    experts = router_weight.shape[1]
    slots = 4 * group // experts // ranks
    hidden = expert_in_weight.shape[2]
    heads_true = qkv_weight.shape[2]
    head_count = heads_true // HDIM
    heads_wide = -(-heads_true // LANES) * LANES
    head_rows = 16
    chunks = 2 if slots >= 32 else 1

    def sent(values, shift):
        return lax.ppermute(values, "mp", [(i, (i + shift) % ranks) for i in range(ranks)])

    def pieces(values):
        return [values] + [sent(values, shift) for shift in range(1, ranks)]

    def exchanged(parts):
        return [sent(parts[shift - 1], shift) for shift in range(1, ranks)]

    def to_experts(rows):
        return lax.all_to_all(rows, "dp", split_axis=0, concat_axis=0, tiled=True)

    def everywhere(values, late):
        for axis, size in (("dp", experts), ("mp", ranks)):
            if axis == "mp":
                values = after(values, *late)
            bit = 1
            while bit < size:
                others = range(bit, 4 * bit if 4 * bit <= size else 2 * bit, bit)
                values = values + sum(
                    lax.ppermute(values, axis, [(i, i ^ other) for i in range(size)])
                    for other in others
                )
                bit *= 1 + len(others)
        return values

    pad_heads = heads_wide - heads_true
    gain_one = norm1_gain.astype(F32).reshape(1, width)
    gain_two = norm2_gain.astype(F32).reshape(1, width)
    out_shard = jnp.pad(attn_out_weight.T, ((0, 0), (0, pad_heads)))
    shard = jnp.concatenate(
        [
            jnp.pad(qkv_weight, ((0, 0), (0, 0), (0, pad_heads))).reshape(-1, 3 * heads_wide),
            *pieces(out_shard),
        ],
        axis=1,
    )
    weights = lax.all_gather(shard, "dp", axis=0, tiled=True)
    out_pieces = [
        weights[:, (3 + piece) * heads_wide : (4 + piece) * heads_wide] for piece in range(ranks)
    ]
    grad_pieces = pieces(cotangent)
    token_pieces = pieces(tokens)
    in_own, out_own = expert_in_weight[0], expert_out_weight[0]
    quarter = hidden // 4
    *in_stacks, own_in_t, in_first, in_second, in_third = lay_call(
        ranks, 0, True, [in_own], [], 0, (quarter, 2 * quarter, quarter)
    )
    *out_stacks, own_out_t, out_whole = lay_call(ranks, 0, False, [out_own], [], 0, (hidden,))
    own_stacks = (expert_in_weight, own_in_t, expert_out_weight, own_out_t)
    in_first = pieces(after(in_first, *token_pieces[1:]))
    in_second = pieces(after(in_second, *in_first[1:]))
    table = lax.dynamic_slice_in_dim(bias_table.T, rank * head_count, head_count, 0)
    table = jnp.pad(table, ((0, head_rows - head_count), (0, LANES - NBUCKET)))
    lookup = jnp.concatenate([jnp.full((1,), -1, jnp.int32), buckets]).reshape(1, 2 * group)
    router = jnp.pad(router_weight, ((0, 0), (0, LANES - experts)))

    by_row, by_col, partners = whole(
        partial(route_kernel, slots),
        [shape((experts, group), F32), shape((group, LANES), F32), shape((experts, 16, LANES), BF)],
        [],
        rank_arr,
        [routes, routes.T],
        0,
    )
    partners = to_experts(partners)
    (grad_rows,) = whole(
        partial(grad_rows_kernel, ranks),
        [shape((experts, slots, width), BF)],
        [pltpu.VMEM((group, width), BF)],
        rank_arr,
        [by_row, *grad_pieces],
        9,
        held=[partners, *token_pieces[1:], *in_stacks, *out_stacks],
    )
    grad_rows = to_experts(after(grad_rows, weights, *in_first[1:]))

    qkv, attended, log_sums, offsets = whole(
        partial(attend_kernel, ranks),
        [
            shape((group, 3 * heads_wide), BF),
            shape((group, heads_wide), BF),
            shape((8, group), F32),
            shape((head_rows, 2 * group), F32),
        ],
        [pltpu.VMEM((2, group // BLOCK, BLOCK, BLOCK), F32)],
        rank_arr,
        [gain_one, weights, table, lookup, *token_pieces],
        16,
    )
    attended_pieces = [attended] + pieces(after(attended, *in_second[1:]))[1:]
    in_third = pieces(after(in_third, *attended_pieces[1:]))
    out_whole = pieces(after(out_whole, *in_third[1:]))
    mid, *send_rows = whole(
        partial(post_kernel, ranks, chunks),
        [shape((own, width), F32)] + [shape((experts, slots // chunks, width), BF)] * chunks,
        [pltpu.VMEM((group, width), BF), pltpu.VMEM((ranks, heads_wide, width), BF)],
        rank_arr,
        [gain_two, by_row, *token_pieces, *attended_pieces, *out_pieces],
        12,
    )
    for piece in range(1, ranks):
        in_parts = [in_first[piece], in_second[piece], in_third[piece]]
        in_stacks = lay_call(ranks, piece, True, in_parts, in_stacks, 4)
    expert_rows = [to_experts(after(send_rows[0], grad_rows, *in_third[1:]))]
    for rows in send_rows[1:]:
        expert_rows.append(to_experts(after(rows, *expert_rows, *in_stacks)))
    own_expert = lax.axis_index("dp").astype(jnp.int32).reshape(1)
    kept, made, results, din_rows = [], [], [], []
    route_grad = jnp.zeros((max(16, experts), width), F32)
    for chunk in range(chunks):
        spans = [(0, 1), (1, ranks)] if chunk == 0 and ranks > 1 else [(0, ranks)]
        sums = []
        for span in spans:
            if span[1] == ranks:
                sums = [*(sums or [None, None]), *results]
            if span[0] == 1:
                for piece in range(1, ranks):
                    arrived = after(out_whole[piece], *sums[:2])
                    out_stacks = lay_call(ranks, piece, False, [arrived], out_stacks, 4)
            stacks = own_stacks if span == (0, 1) else (*in_stacks, *out_stacks)
            kept, made, sums = expert_call(
                own_expert, expert_rows[chunk], grad_rows, partners, router, stacks, chunk,
                chunks, experts, ranks, span, kept, made, sums, 4 if len(spans) > 1 else 35,
            )
        din, route_part, *results = sums
        din_rows.append(to_experts(din))
        route_grad = route_grad + route_part
    (dpart, rows_kept), (act, dpre) = kept, made
    (results,) = results

    def rows_dot(left, right):
        return lax.dot_general(left, right, (((0,), (0,)), ((), ())), preferred_element_type=F32)

    upper = [
        rows_dot(rows_kept[:, : width // 2], dpre[j]).astype(BF) for j in range(1, ranks)
    ]
    lower = [
        rows_dot(rows_kept[:, width // 2 :], dpre[j]).astype(BF) for j in range(1, ranks)
    ]
    out_grads = [rows_dot(act[j], dpart).astype(BF) for j in range(1, ranks)]
    firsts = [sent(grad, ranks - 1 - j) for j, grad in enumerate(upper)]
    seconds = [
        sent(after(grad, *firsts), ranks - 1 - j) for j, grad in enumerate(lower)
    ]
    dmoe_own, dmoe_other = combine_call(
        rank_arr, ranks, by_col, din_rows, own, 8, held=[*firsts, *out_grads]
    )
    dmoe_pieces = exchanged(dmoe_other)
    in_own_grad = rows_dot(after(rows_kept, dmoe_own), dpre[0])
    out_own_grad = rows_dot(act[0], after(dpart, dmoe_own))
    dmid, dbranch, dheads, other_dheads, gain_two_grad = whole(
        partial(mid_back_kernel, ranks),
        [
            shape((own, width), F32),
            shape((own, width), BF),
            shape((own, heads_wide), BF),
            shape((ranks - 1, own, heads_wide), BF),
            shape((1, width), F32),
        ],
        [],
        rank_arr,
        [gain_two, mid, cotangent, dmoe_own, *dmoe_pieces, *out_pieces],
        6,
        held=seconds,
    )
    dheads = [dheads, *exchanged(other_dheads)]
    thirds = [
        sent(after(grad[: 5 * hidden // 8], *dheads[1:]), ranks - 1 - j)
        for j, grad in enumerate(out_grads)
    ]
    early = jnp.concatenate([jnp.pad(gain_two_grad, ((0, 7), (0, 0))), route_grad], axis=0)
    results = to_experts(after(results, *firsts))

    dqkv, table_grad, weight_grad = whole(
        partial(back_and_grad_kernel, ranks, head_count),
        [
            shape((group, 3 * heads_wide), BF),
            shape((16, LANES), F32),
            shape((width, (3 + ranks) * heads_wide), BF),
        ],
        [
            pltpu.VMEM((2, group // BLOCK, BLOCK, BLOCK), F32),
            pltpu.VMEM((2, group // BLOCK, BLOCK, BLOCK), F32),
            pltpu.VMEM((group, heads_wide), BF),
            pltpu.VMEM((group, LANES), F32),
            pltpu.VMEM((group, LANES), F32),
            pltpu.VMEM((head_rows, 2 * group), F32),
            pltpu.VMEM((width, group), BF),
        ],
        rank_arr,
        [
            qkv, log_sums, offsets, lookup, *dheads, gain_one, dbranch, *token_pieces,
            *attended_pieces,
        ],
        29,
        held=[in_own_grad, out_own_grad],
    )
    weight_grad = after(weight_grad, *thirds)
    core = lax.axis_index("dp") % 2
    shards = weight_grad.reshape(experts // 2, 2, width // experts, -1)
    swapped = lax.ppermute(
        lax.dynamic_index_in_dim(shards, 1 - core, 1, keepdims=False),
        "dp",
        [(i, i ^ 1) for i in range(experts)],
    )
    shards = lax.dynamic_index_in_dim(shards, core, 1, keepdims=False)
    shards = (shards.astype(F32) + swapped.astype(F32)).astype(BF)
    dnormed_own, dnormed_other, small = whole(
        partial(project_back_kernel, ranks),
        [
            shape((own, width), F32),
            shape((ranks - 1, own, width), BF),
            shape((24, width), F32),
        ],
        [pltpu.VMEM((1, width), F32), pltpu.VMEM((group, width), F32)],
        rank_arr,
        [weights, dqkv, table_grad, *token_pieces],
        7,
        held=[weight_grad, results],
    )
    dnormed_pieces = exchanged(after(dnormed_other, swapped))
    fourths = [
        sent(after(grad[5 * hidden // 8 :], *dnormed_pieces), ranks - 1 - j)
        for j, grad in enumerate(out_grads)
    ]
    shards = lax.all_to_all(
        shards,
        "dp",
        split_axis=0,
        concat_axis=0,
        tiled=True,
        axis_index_groups=[list(range(start, experts, 2)) for start in range(2)],
    )
    (grad_tokens,) = whole(
        partial(token_back_kernel, ranks),
        [shape((own, width), F32)],
        [],
        rank_arr,
        [gain_one, tokens, dmid, dnormed_own, *dnormed_pieces],
        0,
    )

    weight_total = jnp.sum(shards.astype(F32), axis=0)
    qkv_grad = weight_total[:, : 3 * heads_wide].reshape(-1, 3, heads_wide)[:, :, :heads_true]
    out_part = jnp.split(weight_total[:, 3 * heads_wide :], ranks, axis=1)
    attn_out_grad = out_part[0]
    for shift in range(1, ranks):
        attn_out_grad = attn_out_grad + sent(out_part[shift], ranks - shift)
    attn_out_grad = attn_out_grad[:, :heads_true].T

    moe_own, moe_other = combine_call(
        rank_arr, ranks, by_col, [results], own, 0, held=dnormed_pieces
    )
    small = jnp.concatenate([small, early], axis=0)
    moe_pieces = exchanged(moe_other)
    small = everywhere(after(small, moe_own), [*moe_pieces, *fourths])
    mixed = mid + moe_own
    for piece in moe_pieces:
        mixed = mixed + piece.astype(F32)

    in_grad = add_call(in_own_grad, list(zip(firsts, seconds)))
    out_grad = add_call(out_own_grad, list(zip(thirds, fourths)))
    return (
        mixed.astype(BF),
        grad_tokens,
        small[0],
        qkv_grad,
        attn_out_grad,
        small[8 : 8 + bias_table.shape[1], :NBUCKET].T,
        small[24],
        small[32 : 32 + experts].T,
        in_grad[None],
        out_grad[None],
    )


def solution(mesh):
    placed = (
        P(("dp", "mp"), None),
        P(),
        P("dp", None, "mp"),
        P("mp", "dp"),
        P(),
        P(),
        P(),
        P(),
        P("dp", None),
        P("dp", None, "mp"),
        P("dp", "mp", None),
        P(("dp", "mp"), None),
    )
    return jax.shard_map(
        partial(per_device, mesh.shape["mp"]),
        mesh=mesh,
        in_specs=placed,
        out_specs=(
            P(("dp", "mp"), None),
            P(("dp", "mp"), None),
            P(),
            P("dp", None, "mp"),
            P("mp", "dp"),
            P(),
            P(),
            P(),
            P("dp", None, "mp"),
            P("dp", "mp", None),
        ),
        check_vma=False,
    )
```
